512 devices in a mesh: ctx: 128 (over y, z, core), head: 4 (over x).
Axes of the slice: x: 4, y: 8, z: 8, core: 2. Of those that a mesh axis runs over, the one named last changes fastest.
Arguments:
- queries: bfloat16 [1024, 36864], P('ctx', 'head'), may hold values from -24 to 24
- grad_out: bfloat16 [1024, 32768], P('ctx', 'head'), may hold values from -24 to 24
- latent: bfloat16 [512, 64, 576], P('ctx'), may hold values from -6 to 6
- selected: int32 [128, 32], P('ctx'), may hold values from -1 to 511, as said below
Outputs:
- query_grad: bfloat16 [1024, 36864], P('ctx', 'head')
- latent_grad: bfloat16 [512, 64, 576], P('ctx', None, 'head')
The draws below stay inside these ranges and needn't reach their ends.
Inputs may be any that keep to these rules, and one draw needn't show every extreme that they name: `selected`: entry 0 of row c is c * 4 + 3. Each other entry is -1 or a block of a lower index of ctx (blocks d * 4 .. d * 4 + 3 belong to index d), no two entries of a row on the same index; row c has min(32, c + 1) entries that are not -1, and for c >= 1 one of them is a block of index 0.
All inputs are finite; a program needn't handle non-finite values.
Results may differ from the reference program's by a relative error of at most 0.015.
Values may be sent and summed in bfloat16 or wider, within the bound.
A program may use at most 128 MiB of HBM per device.

```python
import jax
import jax.numpy as jnp
from jax import lax

HEADS = 64
LAT = 576
VDIM = 512
BLK = 64
QBLK = 8
LB_DEV = 4
TOPB = 32
NB = 512
QROWS = 1024
N_CTX = 128
N_HEAD = 4


def latent_base(key):
    keys = jax.random.split(key, 1)
    gauss = jnp.clip(jax.random.normal(keys[0], (NB, BLK, LAT), jnp.float32), -6.0, 6.0)
    base = gauss
    first = base[0]
    even_rows = first[0::2]
    odd_rows = first[1::2]
    paired = jnp.stack([even_rows, odd_rows], axis=1).reshape(BLK, LAT)
    return base.at[0].set(paired)


def draw_latent(key, part):
    shared = latent_base(key)
    return shared.astype(jnp.bfloat16)


def draw_queries(key, part):
    key = jax.random.fold_in(key, 7)
    base = jnp.clip(jax.random.normal(key, (QROWS, HEADS, LAT), jnp.float32), -6.0, 6.0)
    return base.reshape(QROWS, HEADS * LAT).astype(jnp.bfloat16)


def draw_selected(key, part):
    key = jax.random.fold_in(key, 11)
    keys = jax.random.split(key, 2)
    raw = jax.random.randint(keys[0], (N_CTX, N_CTX), 0, 2 ** 20)
    owner = jnp.arange(N_CTX, dtype=jnp.int32)[None, :]
    query_row = jnp.arange(N_CTX, dtype=jnp.int32)[:, None]
    score = raw * N_CTX + owner
    score = jnp.where(owner == 0, 2 ** 28, score)
    score = jnp.where(owner < query_row, score, -(owner + 1))
    values, picked = jax.lax.top_k(score, TOPB - 1)
    inside = jax.random.randint(keys[1], (N_CTX, TOPB - 1), 0, LB_DEV)
    others = jnp.where(values >= 0, picked.astype(jnp.int32) * LB_DEV + inside, -1)
    own = jnp.arange(N_CTX, dtype=jnp.int32) * LB_DEV + LB_DEV - 1
    return jnp.concatenate([own[:, None], others], axis=1).astype(jnp.int32)


def levels(own_key, shape, cuts, low, high):
    gain, own = 1.0, jax.random.fold_in(own_key, 6)
    for axis_at, blocks in cuts:
        steps = jnp.exp(jax.random.uniform(jax.random.fold_in(own, axis_at), (blocks,), jnp.float32, low / len(cuts), high / len(cuts)))
        gain = gain * jnp.repeat(steps, shape[axis_at] // blocks).reshape([-1 if axis == axis_at else 1 for axis in range(len(shape))])
    return gain


def gaussian(stream_key, dims, width, most, pieces=(), kind=jnp.bfloat16):
    loudness = levels(stream_key, dims, pieces, -0.22, 0.18) if pieces else 1.0
    result = jax.random.normal(stream_key, dims, jnp.float32) * width * loudness
    return jnp.minimum(jnp.maximum(result, -most), most).astype(kind)


def setup_inputs(seed: int = 0) -> dict:
    seeds = jax.random.split(jax.random.key(seed), 5)
    return {
        "queries": draw_queries(jax.random.fold_in(seeds[4], 71), 0),
        "grad_out": gaussian(seeds[1], (QROWS, HEADS * VDIM), 4.0, 24.0, ((0, 128), (1, 4))),
        "latent": draw_latent(jax.random.fold_in(seeds[4], 71), 0),
        "selected": draw_selected(jax.random.fold_in(seeds[4], 71), 0),
    }


softmax_scale = 192.0 ** -0.5


def reference(queries, grad_out, latent, selected):
    key_count = TOPB * BLK
    row_count = QBLK * HEADS
    group_heads = HEADS // N_HEAD
    key_slot = jnp.arange(key_count, dtype=jnp.int32) // BLK
    key_pos = jnp.arange(key_count, dtype=jnp.int32) % BLK
    query_pos = BLK - QBLK + jnp.arange(row_count, dtype=jnp.int32) // HEADS

    def step(total, block):
        ids = selected[block]
        safe = jnp.where(ids >= 0, ids, 0)
        keys = latent[safe].reshape(key_count, LAT)
        rows = lax.dynamic_slice_in_dim(queries, block * QBLK, QBLK, 0).reshape(row_count, LAT)
        out_rows = lax.dynamic_slice_in_dim(grad_out, block * QBLK, QBLK, 0).reshape(row_count, VDIM)
        own = block * LB_DEV + LB_DEV - 1
        slot_ids = ids[key_slot]
        seen = (slot_ids[None, :] >= 0) & ((slot_ids[None, :] != own) | (key_pos[None, :] <= query_pos[:, None]))
        scores = softmax_scale * jnp.dot(rows, keys.T, preferred_element_type=jnp.float32)
        top = jnp.max(jnp.where(seen, scores, -jnp.inf), axis=1, keepdims=True)
        weights = jnp.where(seen, jnp.exp(scores - top), 0.0)
        probs = weights / jnp.sum(weights, axis=1, keepdims=True)
        probs16 = probs.astype(jnp.bfloat16)
        values = keys[:, :VDIM]
        dprobs = jnp.dot(out_rows, values.T, preferred_element_type=jnp.float32)
        delta = jnp.sum(probs * dprobs, axis=1, keepdims=True)
        dscores16 = (probs * (dprobs - delta)).astype(jnp.bfloat16)
        query_block = (softmax_scale * jnp.dot(dscores16, keys, preferred_element_type=jnp.float32)).astype(jnp.bfloat16)
        score_groups = dscores16.reshape(QBLK, HEADS, key_count)
        prob_groups = probs16.reshape(QBLK, HEADS, key_count)
        row_groups = rows.reshape(QBLK, HEADS, LAT)
        out_groups = out_rows.reshape(QBLK, HEADS, VDIM)
        key_part = jnp.zeros((key_count, LAT), jnp.float32)
        for group in range(N_HEAD):
            lower = group * group_heads
            upper = lower + group_heads
            group_scores = score_groups[:, lower:upper].reshape(QBLK * group_heads, key_count)
            group_probs = prob_groups[:, lower:upper].reshape(QBLK * group_heads, key_count)
            group_rows = row_groups[:, lower:upper].reshape(QBLK * group_heads, LAT)
            group_outs = out_groups[:, lower:upper].reshape(QBLK * group_heads, VDIM)
            dkeys = softmax_scale * jnp.dot(group_scores.T, group_rows, preferred_element_type=jnp.float32)
            dvalues = jnp.dot(group_probs.T, group_outs, preferred_element_type=jnp.float32)
            partial_value = (dkeys + jnp.pad(dvalues, ((0, 0), (0, LAT - VDIM)))).astype(jnp.bfloat16)
            partial_value = lax.optimization_barrier(partial_value)
            key_part = key_part + partial_value.astype(jnp.float32)
        key_part = key_part.reshape(TOPB, BLK, LAT) * (ids >= 0).astype(jnp.float32)[:, None, None]
        total = total.at[safe].add(key_part)
        return total, query_block.reshape(QBLK, HEADS * LAT)

    start = jnp.zeros((NB, BLK, LAT), jnp.float32)
    total, query_grad = lax.scan(step, start, jnp.arange(N_CTX, dtype=jnp.int32))
    return query_grad.reshape(QROWS, HEADS * LAT), total.astype(jnp.bfloat16)
```

```python
import functools

import jax
import jax.numpy as jnp
from jax import lax
from jax.experimental import pallas as pl
from jax.experimental.pallas import tpu as pltpu
from jax.sharding import PartitionSpec as P

MESH = pl.DeviceIdType.MESH
BF16 = jnp.bfloat16
F32 = jnp.float32
SCALE = 192.0 ** (-0.5)

NY, NZ, NK, NX = 8, 8, 2, 4
RING = 8
BLK, LAT, VDIM = 64, 576, 512
WIDE = 640
ROWS = 288
HALF = 144
QBLK, HEADS_HERE = 8, 16
QR = QBLK * HEADS_HERE
ALLR = QR * NX
SLOTS = 32
CHUNK = 4
CK = CHUNK * BLK
NEG = -1e30
VMEM_LIMIT = 56 * 1024 * 1024

OFFS = (0, -1, 1, -2, 2, -3, 3, -4)
UP = (4, 4, 4, 4, 3, 3, 3, 3)
DOWN = (3, 3, 3, 3, 4, 4, 4, 4)


def where_am_i():
    ctx = lax.axis_index("ctx")
    x = lax.axis_index("head")
    core = lax.rem(ctx, NK)
    chip = ctx // NK
    return lax.rem(chip, NZ), chip // NZ, core, x


def ctx_of(y, z, core):
    return (y * NZ + z) * NK + core


def wrap(v, n):
    return lax.rem(v + 2 * n, n)


def place(half, first, second):
    return second * NZ + first if half == 0 else first * NZ + second


def neighbour(half, ring, step, y, z, core, x):
    along_z = (half == 0) == (ring == 0)
    if along_z:
        return (ctx_of(y, wrap(z + step, NZ), core), x)
    return (ctx_of(wrap(y + step, NY), z, core), x)


def gather_plan():
    plan = []
    for t in range(4):
        plan.append((t, 0, 1, t, 0))
        if t < 3:
            plan.append((t, 0, -1, t, 0))
    for q, off in enumerate(OFFS):
        for s in range(UP[q]):
            plan.append((s + abs(off), 1, 1, s, q))
        for s in range(DOWN[q]):
            plan.append((s + abs(off), 1, -1, s, q))
    return sorted(plan, key=lambda e: (e[0], e[1], -e[3], e[4], -e[2]))


def labels():
    names = {}
    for wave, ring, way, s, q in gather_plan():
        names[(ring, way, s + 1, q)] = len(names)
    return names


LABELS = labels()
NLAB = len(LABELS)


def enter(peers):
    barrier = pltpu.get_barrier_semaphore()
    for peer in peers:
        pl.semaphore_signal(barrier, inc=1, device_id=peer, device_id_type=MESH)
    pl.semaphore_wait(barrier, len(peers))


def ring_peers(y, z, core, x):
    return [neighbour(0, ring, step, y, z, core, x) for ring in (0, 1) for step in (1, -1)]


def group_peers(y, z, core, x):
    me = ctx_of(y, z, core)
    sibling = ctx_of(y, z, 1 - core)
    far = [(me, wrap(x + d, NX)) for d in (1, 2, 3)]
    across = [(sibling, wrap(x + d, NX)) for d in (0, 1, 2, 3)]
    return far, across


def pack_block(block):
    parts = [block[:, 128 * g : 128 * g + 128] for g in range(4)]
    return parts, block[:, VDIM:]


def gather_kernel(
    lat_ref, q_ref, g_ref, sel_ref,
    keys_out, q_out, g_out, sel_out,
    block, pack, qrow, grow, load_sem, local_sem, send_sem, recv_sem, gsend, grecv,
):
    z, y, core, x = where_am_i()
    chip = y * NZ + z
    load = pltpu.make_async_copy(lat_ref.at[x], block, load_sem)
    load.start()
    far, across = group_peers(y, z, core, x)
    enter(ring_peers(y, z, core, x) + far + across[:1])
    load.wait()
    wide = block[...].astype(F32)
    for g in range(4):
        pack[64 * g : 64 * g + 64, :] = block[:, 128 * g : 128 * g + 128]
    tail = jnp.concatenate([wide[:, VDIM:], jnp.zeros((BLK, 64), F32)], axis=1)
    pack[256:288, :] = (tail[:32] + pltpu.roll(tail[32:], 64, axis=1)).astype(BF16)
    keep = pltpu.make_async_copy(pack, keys_out.at[chip], local_sem.at[0])
    keep.start()

    first = {0: z, 1: y}
    second = {0: y, 1: z}
    sends = []
    arrived = set()

    def part(half):
        return pl.ds(HALF * half, HALF)

    def arrival(half, label):
        if (half, label) in arrived:
            return
        arrived.add((half, label))
        pltpu.make_async_copy(
            keys_out.at[chip, part(half)], keys_out.at[chip, part(half)],
            recv_sem.at[half * NLAB + LABELS[label]],
        ).wait()

    def send(half, ring, way, s, q):
        if ring == 0:
            off, along = -way * s, 0
            if s > 0:
                arrival(half, (0, way, s, 0))
        else:
            off, along = OFFS[q], -way * s
            if s > 0:
                arrival(half, (1, way, s, q))
            elif off != 0:
                arrival(half, (0, 1 if off < 0 else -1, abs(off), 0))
        spot = place(half, wrap(first[half] + off, RING), wrap(second[half] + along, RING))
        own = off == 0 and along == 0
        src = pack.at[part(half)] if own else keys_out.at[spot, part(half)]
        number = half * NLAB + LABELS[(ring, way, s + 1, q)]
        copy = pltpu.make_async_remote_copy(
            src_ref=src,
            dst_ref=keys_out.at[spot, part(half)],
            send_sem=send_sem.at[number],
            recv_sem=recv_sem.at[number],
            device_id=neighbour(half, ring, way, y, z, core, x),
            device_id_type=MESH,
        )
        copy.start()
        sends.append(copy)

    plan = gather_plan()
    waves = max(e[0] for e in plan) + 1

    def group_copy(src, out, kind, slot_core, slot_x, peer, number):
        copy = pltpu.make_async_remote_copy(
            src_ref=src,
            dst_ref=out.at[slot_core, slot_x] if kind != 2 else out.at[slot_core],
            send_sem=gsend.at[number],
            recv_sem=grecv.at[number],
            device_id=peer,
            device_id_type=MESH,
        )
        copy.start()
        sends.append(copy)

    group_number = {}

    def number_of(kind, hop):
        return group_number.setdefault((kind, hop), len(group_number))

    def group_arrival(kind, hop):
        ref = (q_out.at[0, 0], g_out.at[0, 0], sel_out.at[0])[kind]
        pltpu.make_async_copy(ref, ref, grecv.at[number_of(kind, hop)]).wait()

    for wave in range(waves):
        for entry in plan:
            if entry[0] == wave:
                for half in (0, 1):
                    send(half, *entry[1:])
        if wave == 0:
            group_copy(sel_ref, sel_out, 2, core, 0, across[0], number_of(2, 0))
            keep_sel = pltpu.make_async_copy(sel_ref, sel_out.at[core], local_sem.at[1])
            keep_sel.start()
            for pair in range(HEADS_HERE // 2):
                both = q_ref[:, 2 * LAT * pair : 2 * LAT * (pair + 1)].astype(F32)
                lane = lax.broadcasted_iota(jnp.int32, (QBLK, WIDE), 1)
                one = jnp.where(lane < LAT, both[:, :WIDE], 0.0)
                two = jnp.where(lane < LAT, pltpu.roll(both[:, VDIM:], WIDE - 64, axis=1), 0.0)
                qrow[16 * pair : 16 * pair + 16, :] = jnp.concatenate([one, two], axis=0).astype(BF16)
                one = g_ref[:, 2 * VDIM * pair : 2 * VDIM * pair + VDIM].astype(F32)
                two = g_ref[:, 2 * VDIM * pair + VDIM : 2 * VDIM * (pair + 1)].astype(F32)
                grow[16 * pair : 16 * pair + 16, :] = jnp.concatenate([one, two], axis=0).astype(BF16)
            for d in range(3):
                group_copy(qrow, q_out, 0, core, x, far[d], number_of(0, 3 - d))
                group_copy(grow, g_out, 1, core, x, far[d], number_of(1, 3 - d))
            group_copy(qrow, q_out, 0, core, x, across[0], number_of(0, 4))
            group_copy(grow, g_out, 1, core, x, across[0], number_of(1, 4))
            keep_q = pltpu.make_async_copy(qrow, q_out.at[core, x], local_sem.at[2])
            keep_q.start()
            keep_g = pltpu.make_async_copy(grow, g_out.at[core, x], local_sem.at[3])
            keep_g.start()
        if wave == 5:
            for d in (1, 3, 2):
                src_x = wrap(x + d, NX)
                group_arrival(0, d)
                group_copy(q_out.at[core, src_x], q_out, 0, core, src_x, across[0], number_of(0, 4 + d))
                group_arrival(1, d)
                group_copy(g_out.at[core, src_x], g_out, 1, core, src_x, across[0], number_of(1, 4 + d))

    for half in (0, 1):
        for label in LABELS:
            arrival(half, label)
    for kind in (0, 1):
        for hop in (4, 5, 6, 7):
            group_arrival(kind, hop)
    group_arrival(2, 0)
    for copy in sends:
        copy.wait_send()
    keep.wait()
    keep_sel.wait()
    keep_q.wait()
    keep_g.wait()


def gather_all(latent, queries, grad_out, selected):
    any_spec = pl.BlockSpec(memory_space=pl.ANY)
    vmem = pl.BlockSpec(memory_space=pltpu.VMEM)
    return pl.pallas_call(
        gather_kernel,
        out_shape=(
            jax.ShapeDtypeStruct((NY * NZ, ROWS, 128), BF16),
            jax.ShapeDtypeStruct((NK, NX, QR, WIDE), BF16),
            jax.ShapeDtypeStruct((NK, NX, QR, VDIM), BF16),
            jax.ShapeDtypeStruct((NK, 1, SLOTS), jnp.int32),
        ),
        in_specs=[any_spec, vmem, vmem, any_spec],
        out_specs=(any_spec, any_spec, any_spec, any_spec),
        scratch_shapes=[
            pltpu.VMEM((BLK, LAT), BF16),
            pltpu.VMEM((ROWS, 128), BF16),
            pltpu.VMEM((QR, WIDE), BF16),
            pltpu.VMEM((QR, VDIM), BF16),
            pltpu.SemaphoreType.DMA(()),
            pltpu.SemaphoreType.DMA((4,)),
            pltpu.SemaphoreType.DMA((2 * NLAB,)),
            pltpu.SemaphoreType.DMA((2 * NLAB,)),
            pltpu.SemaphoreType.DMA((15,)),
            pltpu.SemaphoreType.DMA((15,)),
        ],
        compiler_params=pltpu.CompilerParams(
            collective_id=0, has_side_effects=True, vmem_limit_bytes=VMEM_LIMIT
        ),
        cost_estimate=pl.CostEstimate(flops=0, bytes_accessed=10_000_000, transcendentals=0),
        name="gather_keys",
    )(latent, queries, grad_out, selected)


def list_slots(sel_ref, spots, owns, query_block, kind, own_id):
    def look(j, n):
        block_id = sel_ref[query_block, 0, j]
        mine = (block_id >= 0) & (lax.rem(block_id, 8) == kind)
        spots[n] = jnp.where(mine, block_id // 8, 0)
        owns[n] = jnp.where(mine & (block_id == own_id), 1, 0)
        return n + mine.astype(jnp.int32)

    count = lax.fori_loop(0, SLOTS, look, jnp.int32(0))
    for extra in range(CHUNK):
        spots[count + extra] = 0
        owns[count + extra] = 0
    return count


def load_chunk(chunk, spots, keys_ref, landed, kbuf, sem, slot):
    for i in range(CHUNK):
        pltpu.make_async_copy(
            keys_ref.at[spots[chunk * CHUNK + i]], landed.at[slot, i], sem.at[slot, i]
        ).start()


def take_chunk(keys_ref, landed, kbuf, sem, slot):
    lane = lax.broadcasted_iota(jnp.int32, (32, 128), 1)
    for i in range(CHUNK):
        pltpu.make_async_copy(keys_ref.at[0], landed.at[slot, i], sem.at[slot, i]).wait()
        for g in range(4):
            kbuf[64 * i : 64 * i + 64, 128 * g : 128 * g + 128] = landed[slot, i, 64 * g : 64 * g + 64, :]
        tail = landed[slot, i, 256:288, :].astype(F32)
        kbuf[64 * i : 64 * i + 32, VDIM:] = jnp.where(lane < 64, tail, 0.0).astype(BF16)
        kbuf[64 * i + 32 : 64 * i + 64, VDIM:] = jnp.where(
            lane < 64, pltpu.roll(tail, 64, axis=1), 0.0
        ).astype(BF16)


def seen_of(chunk, owns, count):
    row = lax.broadcasted_iota(jnp.int32, (BLK, ALLR), 0)
    col = lax.broadcasted_iota(jnp.int32, (BLK, ALLR), 1)
    limit = BLK - QBLK + lax.rem(col, QBLK)
    parts = []
    for i in range(CHUNK):
        slot = chunk * CHUNK + i
        top = jnp.where(slot < count, jnp.where(owns[slot] == 1, limit, BLK), -1)
        parts.append(row <= top)
    return jnp.concatenate(parts, axis=0)


def nt(a, b):
    return lax.dot_general(a, b, (((1,), (1,)), ((), ())), preferred_element_type=F32)


def tn(a, b):
    return lax.dot_general(a, b, (((0,), (0,)), ((), ())), preferred_element_type=F32)


def nn(a, b):
    return lax.dot_general(a, b, (((1,), (0,)), ((), ())), preferred_element_type=F32)


def stats_kernel(sel_ref, keys_ref, q_ref, g_ref, stats_ref, landed, kbuf, spots, owns, sem):
    z, y, core, x = where_am_i()
    chip = y * NZ + z
    for qb in range(NK):
        count = list_slots(sel_ref, spots, owns, qb, 4 * core + x, (chip * NK + qb) * 4 + 3)
        chunks = (count + CHUNK - 1) // CHUNK

        @pl.when(chunks > 0)
        def _():
            load_chunk(0, spots, keys_ref, landed, kbuf, sem, 0)

        def step(chunk, carry):
            top, total, delta = carry
            slot = lax.rem(chunk, 2)

            @pl.when(chunk + 1 < chunks)
            def _():
                load_chunk(chunk + 1, spots, keys_ref, landed, kbuf, sem, 1 - slot)

            take_chunk(keys_ref, landed, kbuf, sem, slot)
            seen = seen_of(chunk, owns, count)
            scores = SCALE * nt(kbuf[...], q_ref[qb])
            dprobs = nt(kbuf[:, :VDIM], g_ref[qb])
            scores = jnp.where(seen, scores, NEG)
            new_top = jnp.maximum(top, jnp.max(scores, axis=0, keepdims=True))
            weights = jnp.where(seen, jnp.exp(scores - new_top), 0.0)
            shrink = jnp.exp(top - new_top)
            total = total * shrink + jnp.sum(weights, axis=0, keepdims=True)
            delta = delta * shrink + jnp.sum(weights * dprobs, axis=0, keepdims=True)
            return new_top, total, delta

        zero = jnp.zeros((1, ALLR), F32)
        top, total, delta = lax.fori_loop(0, chunks, step, (zero + NEG, zero, zero))
        stats_ref[qb] = jnp.concatenate([top, total, delta, jnp.zeros((5, ALLR), F32)], axis=0)


def stats_of(sel, keys, queries, grad_out):
    vmem = pl.BlockSpec(memory_space=pltpu.VMEM)
    return pl.pallas_call(
        stats_kernel,
        out_shape=jax.ShapeDtypeStruct((NK, 8, ALLR), F32),
        in_specs=[
            pl.BlockSpec(memory_space=pltpu.SMEM),
            pl.BlockSpec(memory_space=pl.ANY),
            vmem,
            vmem,
        ],
        out_specs=vmem,
        scratch_shapes=[
            pltpu.VMEM((2, CHUNK, ROWS, 128), BF16),
            pltpu.VMEM((CK, WIDE), BF16),
            pltpu.SMEM((SLOTS + CHUNK,), jnp.int32),
            pltpu.SMEM((SLOTS + CHUNK,), jnp.int32),
            pltpu.SemaphoreType.DMA((2, CHUNK)),
        ],
        compiler_params=pltpu.CompilerParams(vmem_limit_bytes=VMEM_LIMIT),
        name="local_stats",
    )(sel, keys, queries, grad_out)


def share_kernel(mine, out, send_sem, recv_sem, local_sem):
    z, y, core, x = where_am_i()
    far, across = group_peers(y, z, core, x)
    enter(far + across)
    slot = x * NK + core
    keep = pltpu.make_async_copy(mine, out.at[slot], local_sem)
    keep.start()
    copies = []
    for number, peer in enumerate(far + across):
        copy = pltpu.make_async_remote_copy(
            src_ref=mine,
            dst_ref=out.at[slot],
            send_sem=send_sem.at[number],
            recv_sem=recv_sem.at[number],
            device_id=peer,
            device_id_type=MESH,
        )
        copy.start()
        copies.append(copy)
    keep.wait()
    for copy in copies:
        copy.wait()


def share_stats(stats):
    vmem = pl.BlockSpec(memory_space=pltpu.VMEM)
    return pl.pallas_call(
        share_kernel,
        out_shape=jax.ShapeDtypeStruct((NX * NK, NK, 8, ALLR), F32),
        in_specs=[vmem],
        out_specs=vmem,
        scratch_shapes=[
            pltpu.SemaphoreType.DMA((7,)),
            pltpu.SemaphoreType.DMA((7,)),
            pltpu.SemaphoreType.DMA(()),
        ],
        compiler_params=pltpu.CompilerParams(collective_id=1, has_side_effects=True),
        name="share_stats",
    )(stats)


def grads_kernel(
    sel_ref, keys_ref, q_ref, g_ref, stats_ref, dkeys_ref, dq_ref, landed, kbuf, dq_acc, spots, owns, sem
):
    z, y, core, x = where_am_i()
    chip = y * NZ + z

    def clear(i, carry):
        dkeys_ref[i] = jnp.zeros((ROWS, 128), BF16)
        return carry

    lax.fori_loop(0, NY * NZ, clear, 0)
    for qb in range(NK):
        count = list_slots(sel_ref, spots, owns, qb, 4 * core + x, (chip * NK + qb) * 4 + 3)
        chunks = (count + CHUNK - 1) // CHUNK

        @pl.when(chunks > 0)
        def _():
            load_chunk(0, spots, keys_ref, landed, kbuf, sem, 0)

        top = stats_ref[0, qb, 0:1, :]
        for d in range(1, NX * NK):
            top = jnp.maximum(top, stats_ref[d, qb, 0:1, :])
        total = jnp.zeros((1, ALLR), F32)
        delta = jnp.zeros((1, ALLR), F32)
        for d in range(NX * NK):
            shrink = jnp.exp(stats_ref[d, qb, 0:1, :] - top)
            total = total + shrink * stats_ref[d, qb, 1:2, :]
            delta = delta + shrink * stats_ref[d, qb, 2:3, :]
        inverse = 1.0 / total
        delta = delta * inverse
        dq_acc[...] = jnp.zeros((ALLR, WIDE), F32)

        def step(chunk, carry):
            slot = lax.rem(chunk, 2)

            @pl.when(chunk + 1 < chunks)
            def _():
                load_chunk(chunk + 1, spots, keys_ref, landed, kbuf, sem, 1 - slot)

            take_chunk(keys_ref, landed, kbuf, sem, slot)
            seen = seen_of(chunk, owns, count)
            scores = SCALE * nt(kbuf[...], q_ref[qb])
            dprobs = nt(kbuf[:, :VDIM], g_ref[qb])
            probs = jnp.where(seen, jnp.exp(jnp.where(seen, scores, NEG) - top), 0.0) * inverse
            probs16 = probs.astype(BF16)
            dscores16 = (probs * (dprobs - delta)).astype(BF16)
            dq_acc[...] += tn(dscores16, kbuf[...])
            dkeys = SCALE * nn(dscores16, q_ref[qb])
            dvalues = nn(probs16, g_ref[qb])
            front = dkeys[:, :VDIM] + dvalues
            back = dkeys[:, VDIM:]
            for i in range(CHUNK):
                slot_now = chunk * CHUNK + i

                @pl.when(slot_now < count)
                def _():
                    spot = spots[slot_now]
                    for g in range(4):
                        old = dkeys_ref[spot, 64 * g : 64 * g + 64, :].astype(F32)
                        new = front[64 * i : 64 * i + 64, 128 * g : 128 * g + 128]
                        dkeys_ref[spot, 64 * g : 64 * g + 64, :] = (old + new).astype(BF16)
                    old = dkeys_ref[spot, 256:288, :].astype(F32)
                    new = back[64 * i : 64 * i + 32] + pltpu.roll(back[64 * i + 32 : 64 * i + 64], 64, axis=1)
                    dkeys_ref[spot, 256:288, :] = (old + new).astype(BF16)

            return carry

        lax.fori_loop(0, chunks, step, 0)
        for g in range(NX):
            dq_ref[qb, g] = (SCALE * dq_acc[QR * g : QR * g + QR, :]).astype(BF16)


def grads_of(sel, keys, queries, grad_out, stats):
    vmem = pl.BlockSpec(memory_space=pltpu.VMEM)
    return pl.pallas_call(
        grads_kernel,
        out_shape=(
            jax.ShapeDtypeStruct((NY * NZ, ROWS, 128), BF16),
            jax.ShapeDtypeStruct((NK, NX, QR, WIDE), BF16),
        ),
        in_specs=[
            pl.BlockSpec(memory_space=pltpu.SMEM),
            pl.BlockSpec(memory_space=pl.ANY),
            vmem,
            vmem,
            vmem,
        ],
        out_specs=(vmem, vmem),
        scratch_shapes=[
            pltpu.VMEM((2, CHUNK, ROWS, 128), BF16),
            pltpu.VMEM((CK, WIDE), BF16),
            pltpu.VMEM((ALLR, WIDE), F32),
            pltpu.SMEM((SLOTS + CHUNK,), jnp.int32),
            pltpu.SMEM((SLOTS + CHUNK,), jnp.int32),
            pltpu.SemaphoreType.DMA((2, CHUNK)),
        ],
        compiler_params=pltpu.CompilerParams(vmem_limit_bytes=VMEM_LIMIT),
        name="local_grads",
    )(sel, keys, queries, grad_out, stats)


def return_kernel(
    dkeys_ref, dq_ref, dq_out, lat_out,
    got, tsum, total, quarters, dq_got, send_sem, recv_sem, qsend, qrecv, lsend, lrecv,
):
    z, y, core, x = where_am_i()
    far, across = group_peers(y, z, core, x)
    peers = far + across
    enter(ring_peers(y, z, core, x) + peers)
    first = {0: z, 1: y}
    second = {0: y, 1: z}
    sends = []

    def part(half):
        return pl.ds(HALF * half, HALF)

    def number(half, ring, way, left, q):
        return half * NLAB + LABELS[(ring, -way, left + 1, q)]

    def arrival(half, ring, way, left, q):
        at = number(half, ring, way, left, q)
        pltpu.make_async_copy(got.at[at], got.at[at], recv_sem.at[at]).wait()
        return at

    def local(half, off, along):
        spot = place(half, wrap(first[half] + off, RING), wrap(second[half] + along, RING))
        return dkeys_ref.at[spot, part(half)]

    def push(src, half, ring, way, left, q):
        at = number(half, ring, way, left, q)
        copy = pltpu.make_async_remote_copy(
            src_ref=src,
            dst_ref=got.at[at],
            send_sem=send_sem.at[at],
            recv_sem=recv_sem.at[at],
            device_id=neighbour(half, ring, way, y, z, core, x),
            device_id_type=MESH,
        )
        copy.start()
        sends.append(copy)

    def row_total(half, q):
        value = local(half, OFFS[q], 0)[...].astype(F32)
        for way in (1, -1):
            at = arrival(half, 1, way, 0, q)
            value = value + got[at].astype(F32)
        return value

    def send_row(half, q):
        off = OFFS[q]
        way, dist = (1, off) if off > 0 else (-1, -off)
        value = row_total(half, q)
        if (0, -way, dist + 1, 0) in LABELS:
            at = arrival(half, 0, way, dist, 0)
            value = value + got[at].astype(F32)
        tsum[half, q] = value.astype(BF16)
        push(tsum.at[half, q], half, 0, way, dist - 1, 0)

    def send_big(half, way, left, q):
        reach = UP[q] if way == -1 else DOWN[q]
        if left == reach - 1:
            push(local(half, OFFS[q], way * (left + 1)), half, 1, way, left, q)
        else:
            at = arrival(half, 1, way, left + 1, q)
            got[at] = (got[at].astype(F32) + local(half, OFFS[q], way * (left + 1))[...].astype(F32)).astype(BF16)
            push(got.at[at], half, 1, way, left, q)

    plan = gather_plan()
    waves = max(e[0] for e in plan) + 1
    for wave in reversed(range(waves)):
        for q, off in enumerate(OFFS):
            if off != 0 and abs(off) - 1 == wave:
                for half in (0, 1):
                    send_row(half, q)
        for entry_wave, ring, way, s, q in plan:
            if ring == 1 and entry_wave == wave:
                for half in (0, 1):
                    send_big(half, -way, s, q)
        if wave == waves - 2:
            for number_here, (ctx, head) in enumerate(peers):
                to_core = core if number_here < 3 else 1 - core
                copy = pltpu.make_async_remote_copy(
                    src_ref=dq_ref.at[to_core, head],
                    dst_ref=dq_got.at[number_here],
                    send_sem=qsend.at[number_here],
                    recv_sem=qrecv.at[number_here],
                    device_id=(ctx, head),
                    device_id_type=MESH,
                )
                copy.start()
                sends.append(copy)

    for half in (0, 1):
        value = row_total(half, 0)
        for way in (1, -1):
            at = arrival(half, 0, way, 0, 0)
            value = value + got[at].astype(F32)
        total[HALF * half : HALF * half + HALF, :] = value

    lane = lax.broadcasted_iota(jnp.int32, (32, 128), 1)
    tail = total[256:288, :]
    low = jnp.where(lane < 64, tail, 0.0)
    high = jnp.where(lane < 64, pltpu.roll(tail, 64, axis=1), 0.0)
    whole = jnp.concatenate(
        [total[64 * g : 64 * g + 64, :] for g in range(4)] + [jnp.concatenate([low, high], axis=0)], axis=1
    )
    for g in range(NX):
        share = LAT // NX
        turned = whole if g == 0 else pltpu.roll(whole, WIDE - share * g, axis=1)
        quarters[g] = turned[:, :share].astype(BF16)
    for d, peer in enumerate(far):
        copy = pltpu.make_async_remote_copy(
            src_ref=quarters.at[peer[1]],
            dst_ref=lat_out.at[x],
            send_sem=lsend.at[d],
            recv_sem=lrecv.at[d],
            device_id=peer,
            device_id_type=MESH,
        )
        copy.start()
        sends.append(copy)
    lat_out[x] = quarters[x]

    for number_here in range(7):
        pltpu.make_async_copy(
            dq_got.at[number_here], dq_got.at[number_here], qrecv.at[number_here]
        ).wait()
    for pair in range(HEADS_HERE // 2):
        rows = pl.ds(16 * pair, 16)
        value = dq_ref[core, x, rows, :].astype(F32)
        for number_here in range(7):
            value = value + dq_got[number_here, rows, :].astype(F32)
        one, two = value[:QBLK], pltpu.roll(value[QBLK:], 64, axis=1)
        dq_out[:, 2 * LAT * pair : 2 * LAT * (pair + 1)] = jnp.concatenate(
            [one[:, :VDIM], one[:, VDIM:] + two[:, :128], two[:, 128:]], axis=1
        ).astype(BF16)
    for d in range(3):
        pltpu.make_async_copy(lat_out.at[0], lat_out.at[0], lrecv.at[d]).wait()
    for copy in sends:
        copy.wait_send()


def return_all(dkeys, dq):
    vmem = pl.BlockSpec(memory_space=pltpu.VMEM)
    return pl.pallas_call(
        return_kernel,
        out_shape=(
            jax.ShapeDtypeStruct((QBLK, HEADS_HERE * LAT), BF16),
            jax.ShapeDtypeStruct((4, BLK, LAT // NX), BF16),
        ),
        in_specs=[vmem, vmem],
        out_specs=(vmem, vmem),
        scratch_shapes=[
            pltpu.VMEM((2 * NLAB, HALF, 128), BF16),
            pltpu.VMEM((2, len(OFFS), HALF, 128), BF16),
            pltpu.VMEM((ROWS, 128), F32),
            pltpu.VMEM((NX, BLK, LAT // NX), BF16),
            pltpu.VMEM((7, QR, WIDE), BF16),
            pltpu.SemaphoreType.DMA((2 * NLAB,)),
            pltpu.SemaphoreType.DMA((2 * NLAB,)),
            pltpu.SemaphoreType.DMA((7,)),
            pltpu.SemaphoreType.DMA((7,)),
            pltpu.SemaphoreType.DMA((3,)),
            pltpu.SemaphoreType.DMA((3,)),
        ],
        compiler_params=pltpu.CompilerParams(
            collective_id=2, has_side_effects=True, vmem_limit_bytes=VMEM_LIMIT
        ),
        cost_estimate=pl.CostEstimate(flops=0, bytes_accessed=10_000_000, transcendentals=0),
        name="return_grads",
    )(dkeys, dq)


def local(queries, grad_out, latent, selected):
    keys, all_q, all_g, sel = gather_all(latent, queries, grad_out, selected)
    all_q = all_q.reshape(NK, ALLR, WIDE)
    all_g = all_g.reshape(NK, ALLR, VDIM)
    stats = share_stats(stats_of(sel, keys, all_q, all_g))
    dkeys, dq = grads_of(sel, keys, all_q, all_g, stats)
    return return_all(dkeys, dq)


def solution(mesh):
    placed = (P("ctx", "head"), P("ctx", "head"), P("ctx", None, None), P("ctx", None))
    return jax.shard_map(
        local,
        mesh=mesh,
        in_specs=placed,
        out_specs=(P("ctx", "head"), P("ctx", None, "head")),
        check_vma=False,
    )
```

```python
import functools

import jax
import jax.numpy as jnp
from jax import lax
from jax.experimental import pallas as pl
from jax.experimental.pallas import tpu as pltpu
from jax.sharding import PartitionSpec as P

MESH = pl.DeviceIdType.MESH
BF16 = jnp.bfloat16
F32 = jnp.float32
SCALE = 192.0 ** (-0.5)

NY, NZ, NK, NX = 8, 8, 2, 4
RING = 8
BLK, LAT, VDIM = 64, 576, 512
WIDE = 640
ROWS = 288
HALF = 144
QBLK, HEADS_HERE = 8, 16
QR = QBLK * HEADS_HERE
ALLR = QR * NX
SLOTS = 32
CHUNK = 4
CK = CHUNK * BLK
NEG = -1e30
VMEM_LIMIT = 56 * 1024 * 1024

OFFS = (0, -1, 1, -2, 2, -3, 3, -4)
UP = (4, 4, 4, 4, 3, 3, 3, 3)
DOWN = (3, 3, 3, 3, 4, 4, 4, 4)


def where_am_i():
    ctx = lax.axis_index("ctx")
    x = lax.axis_index("head")
    core = lax.rem(ctx, NK)
    chip = ctx // NK
    return lax.rem(chip, NZ), chip // NZ, core, x


def ctx_of(y, z, core):
    return (y * NZ + z) * NK + core


def wrap(v, n):
    return lax.rem(v + 2 * n, n)


def place(half, first, second):
    return second * NZ + first if half == 0 else first * NZ + second


def neighbour(half, ring, step, y, z, core, x):
    along_z = (half == 0) == (ring == 0)
    if along_z:
        return (ctx_of(y, wrap(z + step, NZ), core), x)
    return (ctx_of(wrap(y + step, NY), z, core), x)


READY, WORK = 15.0, 0.5
PASS = ((6.0, (0, 3)), (6.2, (1, 1)), (9.0, (1, 3)), (9.2, (0, 1)), (12.0, (0, 2)), (12.2, (1, 2)))
PIECE, DELAY = 0.72, 1.5


def gather_plan():
    sends = {}
    for half in (0, 1):
        for t in range(4):
            sends[(half, 0, 1, t, 0)] = (half, 0, 1, t - 1, 0) if t else None
        for t in range(3):
            sends[(half, 0, -1, t, 0)] = (half, 0, -1, t - 1, 0) if t else None
        for q, off in enumerate(OFFS):
            root = (half, 0, 1 if off < 0 else -1, abs(off) - 1, 0) if off else None
            for s in range(UP[q]):
                sends[(half, 1, 1, s, q)] = (half, 1, 1, s - 1, q) if s else root
            for s in range(DOWN[q]):
                sends[(half, 1, -1, s, q)] = (half, 1, -1, s - 1, q) if s else root
    left = {}
    for key in sends:
        length, at = 0, key
        while at is not None:
            left[at] = max(left.get(at, 0), length)
            length, at = length + 1, sends[at]
    free, ready, order = {}, {k: 0.0 for k in sends if sends[k] is None}, []

    def link(key):
        return (key[0] ^ key[1], key[2])

    while ready:
        at = min(ready, key=lambda k: (round(max(ready[k], free.get(link(k), 0.0)), 3), -left[k], k))
        since = ready.pop(at)
        begin = max(since, free.get(link(at), 0.0))
        free[link(at)] = begin + PIECE
        order.append((begin, since, at))
        for key, root in sends.items():
            if root == at:
                ready[key] = begin + PIECE + DELAY
    return order


def labels():
    names = {}
    for begin, since, (half, ring, way, s, q) in gather_plan():
        if half == 0:
            names[(ring, way, s + 1, q)] = len(names)
    return names


LABELS = labels()


def route(half, dy, dz):
    off, along = (dz, dy) if half == 0 else (dy, dz)
    if along == 0:
        return None if off == 0 else (0, 1 if off < 0 else -1, abs(off), 0)
    q = OFFS.index(off)
    if along == -4 and UP[q] < 4:
        return (1, -1, 4, q)
    return (1, 1 if along < 0 else -1, abs(along), q)


def gather_steps():
    lands = {(None, 0): 0.0, (None, 1): 0.0}
    for begin, since, (half, ring, way, s, q) in gather_plan():
        lands[((ring, way, s + 1, q), half)] = begin + PIECE + DELAY
    blocks = []
    for dy in OFFS:
        for dz in OFFS:
            blocks.append((max(lands[(route(half, dy, dz), half)] for half in (0, 1)), dy, dz))
    blocks.sort(key=lambda b: (b[0], abs(b[1]) + abs(b[2]), b))
    work, clock = [], READY
    for first in range(0, len(blocks), CHUNK):
        group = blocks[first : first + CHUNK]
        clock = max(clock, group[-1][0] * 1.15 + 0.5)
        for qb in range(NK):
            work.append((clock, qb, [b[1:] for b in group]))
            clock = clock + WORK
    sends = gather_plan()
    merged = []
    marks = [(1.0, "start")] + [(t, "pass") + what for t, what in PASS] + [(t, "work", qb, group) for t, qb, group in work]
    marks.sort(key=lambda m: m[0])
    for mark in marks:
        for entry in [e for e in sends if e[1] * 1.15 + 0.5 <= mark[0] or mark[1] in ('start', 'pass') and e[1] <= mark[0]]:
            merged.append(("send", entry[2]))
            sends.remove(entry)
        merged.append(mark[1:])
    return merged + [("send", entry[2]) for entry in sends]
NLAB = len(LABELS)


def enter(peers):
    barrier = pltpu.get_barrier_semaphore()
    for peer in peers:
        pl.semaphore_signal(barrier, inc=1, device_id=peer, device_id_type=MESH)
    pl.semaphore_wait(barrier, len(peers))


def ring_peers(y, z, core, x):
    return [neighbour(0, ring, step, y, z, core, x) for ring in (0, 1) for step in (1, -1)]


def group_peers(y, z, core, x):
    me = ctx_of(y, z, core)
    sibling = ctx_of(y, z, 1 - core)
    far = [(me, wrap(x + d, NX)) for d in (1, 2, 3)]
    across = [(sibling, wrap(x + d, NX)) for d in (0, 1, 2, 3)]
    return far, across


def pack_block(block):
    parts = [block[:, 128 * g : 128 * g + 128] for g in range(4)]
    return parts, block[:, VDIM:]


def gather_kernel(
    lat_ref, q_ref, g_ref, sel_ref,
    keys_final, q_final, g_final, sel_final, stats_all,
    keys_out, q_out, g_out, sel_out, block, pack, qrow, grow, stats, unseen,
    load_sem, local_sem, out_sem, send_sem, recv_sem, gsend, grecv, ssend, srecv,
):
    z, y, core, x = where_am_i()
    chip = y * NZ + z
    load = pltpu.make_async_copy(lat_ref.at[x], block, load_sem)
    load.start()
    far, across = group_peers(y, z, core, x)
    enter(ring_peers(y, z, core, x) + far + across)
    load.wait()
    wide = block[...].astype(F32)
    for g in range(4):
        pack[64 * g : 64 * g + 64, :] = block[:, 128 * g : 128 * g + 128]
    tail = jnp.concatenate([wide[:, VDIM:], jnp.zeros((BLK, 64), F32)], axis=1)
    pack[256:288, :] = (tail[:32] + pltpu.roll(tail[32:], 64, axis=1)).astype(BF16)
    keep = pltpu.make_async_copy(pack, keys_out.at[chip], local_sem.at[0])
    keep.start()

    first = {0: z, 1: y}
    second = {0: y, 1: z}
    sends = []
    arrived = set()

    def part(half):
        return pl.ds(HALF * half, HALF)

    def arrival(half, label):
        if (half, label) in arrived:
            return
        arrived.add((half, label))
        pltpu.make_async_copy(
            keys_out.at[chip, part(half)], keys_out.at[chip, part(half)],
            recv_sem.at[half * NLAB + LABELS[label]],
        ).wait()

    def send(half, ring, way, s, q):
        if ring == 0:
            off, along = -way * s, 0
            if s > 0:
                arrival(half, (0, way, s, 0))
        else:
            off, along = OFFS[q], -way * s
            if s > 0:
                arrival(half, (1, way, s, q))
            elif off != 0:
                arrival(half, (0, 1 if off < 0 else -1, abs(off), 0))
        spot = place(half, wrap(first[half] + off, RING), wrap(second[half] + along, RING))
        own = off == 0 and along == 0
        src = pack.at[part(half)] if own else keys_out.at[spot, part(half)]
        number = half * NLAB + LABELS[(ring, way, s + 1, q)]
        copy = pltpu.make_async_remote_copy(
            src_ref=src,
            dst_ref=keys_out.at[spot, part(half)],
            send_sem=send_sem.at[number],
            recv_sem=recv_sem.at[number],
            device_id=neighbour(half, ring, way, y, z, core, x),
            device_id_type=MESH,
        )
        copy.start()
        sends.append(copy)

    def group_copy(src, out, kind, slot_core, slot_x, peer, number):
        copy = pltpu.make_async_remote_copy(
            src_ref=src,
            dst_ref=out.at[slot_core, slot_x] if kind != 2 else out.at[slot_core],
            send_sem=gsend.at[number],
            recv_sem=grecv.at[number],
            device_id=peer,
            device_id_type=MESH,
        )
        copy.start()
        sends.append(copy)

    group_number = {}

    def number_of(kind, hop):
        return group_number.setdefault((kind, hop), len(group_number))

    def group_arrival(kind, hop):
        ref = (q_out.at[0, 0], g_out.at[0, 0], sel_out.at[0])[kind]
        pltpu.make_async_copy(ref, ref, grecv.at[number_of(kind, hop)]).wait()

    def start_group():
        group_copy(sel_ref, sel_out, 2, core, 0, across[0], number_of(2, 0))
        keep_sel.start()
        for pair in range(HEADS_HERE // 2):
            both = q_ref[:, 2 * LAT * pair : 2 * LAT * (pair + 1)].astype(F32)
            lane = lax.broadcasted_iota(jnp.int32, (QBLK, WIDE), 1)
            one = jnp.where(lane < LAT, both[:, :WIDE], 0.0)
            two = jnp.where(lane < LAT, pltpu.roll(both[:, VDIM:], WIDE - 64, axis=1), 0.0)
            qrow[16 * pair : 16 * pair + 16, :] = jnp.concatenate([one, two], axis=0).astype(BF16)
            one = g_ref[:, 2 * VDIM * pair : 2 * VDIM * pair + VDIM].astype(F32)
            two = g_ref[:, 2 * VDIM * pair + VDIM : 2 * VDIM * (pair + 1)].astype(F32)
            grow[16 * pair : 16 * pair + 16, :] = jnp.concatenate([one, two], axis=0).astype(BF16)
        group_copy(qrow, q_out, 0, core, x, far[0], number_of(0, 3))
        group_copy(grow, g_out, 1, core, x, far[2], number_of(1, 1))
        group_copy(qrow, q_out, 0, core, x, across[0], number_of(0, 4))
        group_copy(grow, g_out, 1, core, x, across[0], number_of(1, 4))
        group_copy(grow, g_out, 1, core, x, far[0], number_of(1, 3))
        group_copy(qrow, q_out, 0, core, x, far[2], number_of(0, 1))
        keep_q.start()
        keep_g.start()

    def pass_on(kind, hop):
        src_x = wrap(x + hop, NX)
        group_arrival(kind, hop)
        out = (q_out, g_out)[kind]
        if (kind, hop) == (0, 3):
            group_copy(out.at[core, src_x], out, kind, core, src_x, far[0], number_of(kind, 2))
        if (kind, hop) == (1, 1):
            group_copy(out.at[core, src_x], out, kind, core, src_x, far[2], number_of(kind, 2))
        group_copy(out.at[core, src_x], out, kind, core, src_x, across[0], number_of(kind, 4 + hop))

    keep_sel = pltpu.make_async_copy(sel_ref, sel_out.at[core], local_sem.at[1])
    keep_q = pltpu.make_async_copy(qrow, q_out.at[core, x], local_sem.at[2])
    keep_g = pltpu.make_async_copy(grow, g_out.at[core, x], local_sem.at[3])
    finals = [
        pltpu.make_async_copy(q_out, q_final, local_sem.at[4]),
        pltpu.make_async_copy(g_out, g_final, local_sem.at[5]),
        pltpu.make_async_copy(sel_out, sel_final, local_sem.at[6]),
    ]

    def group_done():
        for kind in (0, 1):
            for hop in (4, 5, 6, 7):
                group_arrival(kind, hop)
        group_arrival(2, 0)
        keep_sel.wait()
        keep_q.wait()
        keep_g.wait()
        for copy in finals:
            copy.start()
        ids = lax.broadcasted_iota(jnp.int32, (NY * NZ, SLOTS), 0) * 8 + 4 * core + x
        for qb in range(NK):
            hit = jnp.max(jnp.where(sel_out[qb] == ids, 1.0, 0.0), axis=1, keepdims=True)
            unseen[qb] = jnp.broadcast_to(jnp.where(hit > 0.0, 0.0, NEG), (NY * NZ, 128))
            stats[3 * qb : 3 * qb + 3, :] = jnp.concatenate(
                [jnp.full((1, ALLR), NEG, F32), jnp.zeros((2, ALLR), F32)], axis=0
            )

    lane = lax.broadcasted_iota(jnp.int32, (32, 128), 1)

    def work(qb, group):
        fronts, tails, hides = [], [], []
        for dy, dz in group:
            for half in (0, 1):
                label = route(half, dy, dz)
                if label is not None:
                    arrival(half, label)
            spot = wrap(y + dy, NY) * NZ + wrap(z + dz, NZ)
            if (dy, dz) == (0, 0) and qb == 0:
                keep.wait()
            if qb == 0:
                pltpu.make_async_copy(keys_out.at[spot], keys_final.at[spot], out_sem).start()
            fronts.append(jnp.concatenate([keys_out[spot, 64 * g : 64 * g + 64, :] for g in range(4)], axis=1))
            tail = keys_out[spot, 256:288, :].astype(F32)
            low = jnp.where(lane < 64, tail, 0.0)
            high = jnp.where(lane < 64, pltpu.roll(tail, 64, axis=1), 0.0)
            tails.append(jnp.concatenate([low, high], axis=0).astype(BF16))
            hide = jnp.concatenate([unseen[qb, pl.ds(spot, 1), :]] * 4, axis=1)
            hide = jnp.broadcast_to(hide, (BLK, ALLR))
            if (dy, dz) == (0, 0):
                row = lax.broadcasted_iota(jnp.int32, (BLK, ALLR), 0)
                col = lax.broadcasted_iota(jnp.int32, (BLK, ALLR), 1)
                late = row > BLK - QBLK + lax.rem(col, QBLK)
                own = (x == NX - 1) & (core == qb)
                hide = jnp.where(late & own, NEG, hide)
            hides.append(hide)
        front = jnp.concatenate(fronts, axis=0)
        whole = jnp.concatenate([front, jnp.concatenate(tails, axis=0)], axis=1)
        scores = SCALE * nt(whole, q_out[qb].reshape(ALLR, WIDE)) + jnp.concatenate(hides, axis=0)
        dprobs = nt(front, g_out[qb].reshape(ALLR, VDIM))
        top = stats[3 * qb : 3 * qb + 1, :]
        new_top = jnp.maximum(top, jnp.max(scores, axis=0, keepdims=True))
        weights = jnp.exp(scores - new_top)
        shrink = jnp.exp(top - new_top)
        total = stats[3 * qb + 1 : 3 * qb + 2, :] * shrink + jnp.sum(weights, axis=0, keepdims=True)
        delta = stats[3 * qb + 2 : 3 * qb + 3, :] * shrink + jnp.sum(weights * dprobs, axis=0, keepdims=True)
        stats[3 * qb : 3 * qb + 3, :] = jnp.concatenate([new_top, total, delta], axis=0)

    stats[...] = jnp.zeros((8, ALLR), F32)
    begun = False
    for mark in gather_steps():
        if mark[0] == "send":
            send(*mark[1])
        elif mark[0] == "start":
            start_group()
        elif mark[0] == "pass":
            pass_on(*mark[1:])
        else:
            if not begun:
                group_done()
                begun = True
            work(*mark[1:])

    slot = x * NK + core
    for number, peer in enumerate(far + across):
        copy = pltpu.make_async_remote_copy(
            src_ref=stats,
            dst_ref=stats_all.at[slot],
            send_sem=ssend.at[number],
            recv_sem=srecv.at[number],
            device_id=peer,
            device_id_type=MESH,
        )
        copy.start()
        sends.append(copy)
    stats_all[slot] = stats[...]
    for number in range(7):
        pltpu.make_async_copy(stats_all.at[0], stats_all.at[0], srecv.at[number]).wait()
    for copy in sends:
        copy.wait_send()
    for copy in finals:
        copy.wait()
    pltpu.make_async_copy(keys_out, keys_final, out_sem).wait()


def gather_all(latent, queries, grad_out, selected):
    any_spec = pl.BlockSpec(memory_space=pl.ANY)
    vmem = pl.BlockSpec(memory_space=pltpu.VMEM)
    return pl.pallas_call(
        gather_kernel,
        out_shape=(
            jax.ShapeDtypeStruct((NY * NZ, ROWS, 128), BF16),
            jax.ShapeDtypeStruct((NK, NX, QR, WIDE), BF16),
            jax.ShapeDtypeStruct((NK, NX, QR, VDIM), BF16),
            jax.ShapeDtypeStruct((NK, 1, SLOTS), jnp.int32),
            jax.ShapeDtypeStruct((NX * NK, 8, ALLR), F32),
        ),
        in_specs=[any_spec, vmem, vmem, any_spec],
        out_specs=(any_spec, any_spec, any_spec, any_spec, vmem),
        scratch_shapes=[
            pltpu.VMEM((NY * NZ, ROWS, 128), BF16),
            pltpu.VMEM((NK, NX, QR, WIDE), BF16),
            pltpu.VMEM((NK, NX, QR, VDIM), BF16),
            pltpu.VMEM((NK, 1, SLOTS), jnp.int32),
            pltpu.VMEM((BLK, LAT), BF16),
            pltpu.VMEM((ROWS, 128), BF16),
            pltpu.VMEM((QR, WIDE), BF16),
            pltpu.VMEM((QR, VDIM), BF16),
            pltpu.VMEM((8, ALLR), F32),
            pltpu.VMEM((NK, NY * NZ, 128), F32),
            pltpu.SemaphoreType.DMA(()),
            pltpu.SemaphoreType.DMA((7,)),
            pltpu.SemaphoreType.DMA(()),
            pltpu.SemaphoreType.DMA((2 * NLAB,)),
            pltpu.SemaphoreType.DMA((2 * NLAB,)),
            pltpu.SemaphoreType.DMA((15,)),
            pltpu.SemaphoreType.DMA((15,)),
            pltpu.SemaphoreType.DMA((7,)),
            pltpu.SemaphoreType.DMA((7,)),
        ],
        compiler_params=pltpu.CompilerParams(
            collective_id=0, has_side_effects=True, vmem_limit_bytes=VMEM_LIMIT
        ),
        cost_estimate=pl.CostEstimate(flops=0, bytes_accessed=10_000_000, transcendentals=0),
        name="gather_keys",
    )(latent, queries, grad_out, selected)


def list_slots(sel_ref, spots, owns, query_block, kind, own_id):
    def look(j, n):
        block_id = sel_ref[query_block, 0, j]
        mine = (block_id >= 0) & (lax.rem(block_id, 8) == kind)
        spots[n] = jnp.where(mine, block_id // 8, 0)
        owns[n] = jnp.where(mine & (block_id == own_id), 1, 0)
        return n + mine.astype(jnp.int32)

    count = lax.fori_loop(0, SLOTS, look, jnp.int32(0))
    for extra in range(CHUNK):
        spots[count + extra] = 0
        owns[count + extra] = 0
    return count


def load_chunk(chunk, spots, keys_ref, landed, kbuf, sem, slot):
    for i in range(CHUNK):
        pltpu.make_async_copy(
            keys_ref.at[spots[chunk * CHUNK + i]], landed.at[slot, i], sem.at[slot, i]
        ).start()


def take_chunk(keys_ref, landed, kbuf, sem, slot):
    lane = lax.broadcasted_iota(jnp.int32, (32, 128), 1)
    for i in range(CHUNK):
        pltpu.make_async_copy(keys_ref.at[0], landed.at[slot, i], sem.at[slot, i]).wait()
        for g in range(4):
            kbuf[64 * i : 64 * i + 64, 128 * g : 128 * g + 128] = landed[slot, i, 64 * g : 64 * g + 64, :]
        tail = landed[slot, i, 256:288, :].astype(F32)
        kbuf[64 * i : 64 * i + 32, VDIM:] = jnp.where(lane < 64, tail, 0.0).astype(BF16)
        kbuf[64 * i + 32 : 64 * i + 64, VDIM:] = jnp.where(
            lane < 64, pltpu.roll(tail, 64, axis=1), 0.0
        ).astype(BF16)


def seen_of(chunk, owns, count):
    row = lax.broadcasted_iota(jnp.int32, (BLK, ALLR), 0)
    col = lax.broadcasted_iota(jnp.int32, (BLK, ALLR), 1)
    limit = BLK - QBLK + lax.rem(col, QBLK)
    parts = []
    for i in range(CHUNK):
        slot = chunk * CHUNK + i
        top = jnp.where(slot < count, jnp.where(owns[slot] == 1, limit, BLK), -1)
        parts.append(row <= top)
    return jnp.concatenate(parts, axis=0)


def nt(a, b):
    return lax.dot_general(a, b, (((1,), (1,)), ((), ())), preferred_element_type=F32)


def tn(a, b):
    return lax.dot_general(a, b, (((0,), (0,)), ((), ())), preferred_element_type=F32)


def nn(a, b):
    return lax.dot_general(a, b, (((1,), (0,)), ((), ())), preferred_element_type=F32)


def grads_kernel(
    sel_ref, keys_ref, q_ref, g_ref, stats_ref, dkeys_ref, dq_ref, landed, kbuf, dq_acc, spots, owns, sem
):
    z, y, core, x = where_am_i()
    chip = y * NZ + z

    def clear(i, carry):
        dkeys_ref[i] = jnp.zeros((ROWS, 128), BF16)
        return carry

    lax.fori_loop(0, NY * NZ, clear, 0)
    for qb in range(NK):
        count = list_slots(sel_ref, spots, owns, qb, 4 * core + x, (chip * NK + qb) * 4 + 3)
        chunks = (count + CHUNK - 1) // CHUNK

        @pl.when(chunks > 0)
        def _():
            load_chunk(0, spots, keys_ref, landed, kbuf, sem, 0)

        top = stats_ref[0, 3 * qb : 3 * qb + 1, :]
        for d in range(1, NX * NK):
            top = jnp.maximum(top, stats_ref[d, 3 * qb : 3 * qb + 1, :])
        total = jnp.zeros((1, ALLR), F32)
        delta = jnp.zeros((1, ALLR), F32)
        for d in range(NX * NK):
            shrink = jnp.exp(stats_ref[d, 3 * qb : 3 * qb + 1, :] - top)
            total = total + shrink * stats_ref[d, 3 * qb + 1 : 3 * qb + 2, :]
            delta = delta + shrink * stats_ref[d, 3 * qb + 2 : 3 * qb + 3, :]
        inverse = 1.0 / total
        delta = delta * inverse
        dq_acc[...] = jnp.zeros((ALLR, WIDE), F32)

        def step(chunk, carry):
            slot = lax.rem(chunk, 2)

            @pl.when(chunk + 1 < chunks)
            def _():
                load_chunk(chunk + 1, spots, keys_ref, landed, kbuf, sem, 1 - slot)

            take_chunk(keys_ref, landed, kbuf, sem, slot)
            seen = seen_of(chunk, owns, count)
            scores = SCALE * nt(kbuf[...], q_ref[qb])
            dprobs = nt(kbuf[:, :VDIM], g_ref[qb])
            probs = jnp.where(seen, jnp.exp(jnp.where(seen, scores, NEG) - top), 0.0) * inverse
            probs16 = probs.astype(BF16)
            dscores16 = (probs * (dprobs - delta)).astype(BF16)
            dq_acc[...] += tn(dscores16, kbuf[...])
            dkeys = SCALE * nn(dscores16, q_ref[qb])
            dvalues = nn(probs16, g_ref[qb])
            front = dkeys[:, :VDIM] + dvalues
            back = dkeys[:, VDIM:]
            for i in range(CHUNK):
                slot_now = chunk * CHUNK + i

                @pl.when(slot_now < count)
                def _():
                    spot = spots[slot_now]
                    for g in range(4):
                        old = dkeys_ref[spot, 64 * g : 64 * g + 64, :].astype(F32)
                        new = front[64 * i : 64 * i + 64, 128 * g : 128 * g + 128]
                        dkeys_ref[spot, 64 * g : 64 * g + 64, :] = (old + new).astype(BF16)
                    old = dkeys_ref[spot, 256:288, :].astype(F32)
                    new = back[64 * i : 64 * i + 32] + pltpu.roll(back[64 * i + 32 : 64 * i + 64], 64, axis=1)
                    dkeys_ref[spot, 256:288, :] = (old + new).astype(BF16)

            return carry

        lax.fori_loop(0, chunks, step, 0)
        for g in range(NX):
            dq_ref[qb, g] = (SCALE * dq_acc[QR * g : QR * g + QR, :]).astype(BF16)


def grads_of(sel, keys, queries, grad_out, stats):
    vmem = pl.BlockSpec(memory_space=pltpu.VMEM)
    return pl.pallas_call(
        grads_kernel,
        out_shape=(
            jax.ShapeDtypeStruct((NY * NZ, ROWS, 128), BF16),
            jax.ShapeDtypeStruct((NK, NX, QR, WIDE), BF16),
        ),
        in_specs=[
            pl.BlockSpec(memory_space=pltpu.SMEM),
            pl.BlockSpec(memory_space=pl.ANY),
            vmem,
            vmem,
            vmem,
        ],
        out_specs=(vmem, vmem),
        scratch_shapes=[
            pltpu.VMEM((2, CHUNK, ROWS, 128), BF16),
            pltpu.VMEM((CK, WIDE), BF16),
            pltpu.VMEM((ALLR, WIDE), F32),
            pltpu.SMEM((SLOTS + CHUNK,), jnp.int32),
            pltpu.SMEM((SLOTS + CHUNK,), jnp.int32),
            pltpu.SemaphoreType.DMA((2, CHUNK)),
        ],
        compiler_params=pltpu.CompilerParams(vmem_limit_bytes=VMEM_LIMIT),
        name="local_grads",
    )(sel, keys, queries, grad_out, stats)


def return_kernel(
    dkeys_ref, dq_ref, dq_out, lat_out,
    got, tsum, total, quarters, dq_got, send_sem, recv_sem, qsend, qrecv, lsend, lrecv,
):
    z, y, core, x = where_am_i()
    far, across = group_peers(y, z, core, x)
    peers = far + across
    enter(ring_peers(y, z, core, x) + peers)
    first = {0: z, 1: y}
    second = {0: y, 1: z}
    sends = []

    def part(half):
        return pl.ds(HALF * half, HALF)

    def number(half, ring, way, left, q):
        return half * NLAB + LABELS[(ring, -way, left + 1, q)]

    def arrival(half, ring, way, left, q):
        at = number(half, ring, way, left, q)
        pltpu.make_async_copy(got.at[at], got.at[at], recv_sem.at[at]).wait()
        return at

    def local(half, off, along):
        spot = place(half, wrap(first[half] + off, RING), wrap(second[half] + along, RING))
        return dkeys_ref.at[spot, part(half)]

    def push(src, half, ring, way, left, q):
        at = number(half, ring, way, left, q)
        copy = pltpu.make_async_remote_copy(
            src_ref=src,
            dst_ref=got.at[at],
            send_sem=send_sem.at[at],
            recv_sem=recv_sem.at[at],
            device_id=neighbour(half, ring, way, y, z, core, x),
            device_id_type=MESH,
        )
        copy.start()
        sends.append(copy)

    def row_total(half, q):
        value = local(half, OFFS[q], 0)[...].astype(F32)
        for way in (1, -1):
            at = arrival(half, 1, way, 0, q)
            value = value + got[at].astype(F32)
        return value

    def send_row(half, q):
        off = OFFS[q]
        way, dist = (1, off) if off > 0 else (-1, -off)
        value = row_total(half, q)
        if (0, -way, dist + 1, 0) in LABELS:
            at = arrival(half, 0, way, dist, 0)
            value = value + got[at].astype(F32)
        tsum[half, q] = value.astype(BF16)
        push(tsum.at[half, q], half, 0, way, dist - 1, 0)

    def send_big(half, way, left, q):
        reach = UP[q] if way == -1 else DOWN[q]
        if left == reach - 1:
            push(local(half, OFFS[q], way * (left + 1)), half, 1, way, left, q)
        else:
            at = arrival(half, 1, way, left + 1, q)
            got[at] = (got[at].astype(F32) + local(half, OFFS[q], way * (left + 1))[...].astype(F32)).astype(BF16)
            push(got.at[at], half, 1, way, left, q)

    for turn, (begin, since, (half, ring, way, s, q)) in enumerate(reversed(gather_plan())):
        if ring == 0:
            send_row(half, OFFS.index(-way * (s + 1)))
        else:
            send_big(half, -way, s, q)
        if turn == 24:
            for number_here, (ctx, head) in enumerate(peers):
                to_core = core if number_here < 3 else 1 - core
                copy = pltpu.make_async_remote_copy(
                    src_ref=dq_ref.at[to_core, head],
                    dst_ref=dq_got.at[number_here],
                    send_sem=qsend.at[number_here],
                    recv_sem=qrecv.at[number_here],
                    device_id=(ctx, head),
                    device_id_type=MESH,
                )
                copy.start()
                sends.append(copy)

    for half in (0, 1):
        value = row_total(half, 0)
        for way in (1, -1):
            at = arrival(half, 0, way, 0, 0)
            value = value + got[at].astype(F32)
        total[HALF * half : HALF * half + HALF, :] = value

    lane = lax.broadcasted_iota(jnp.int32, (32, 128), 1)
    tail = total[256:288, :]
    low = jnp.where(lane < 64, tail, 0.0)
    high = jnp.where(lane < 64, pltpu.roll(tail, 64, axis=1), 0.0)
    whole = jnp.concatenate(
        [total[64 * g : 64 * g + 64, :] for g in range(4)] + [jnp.concatenate([low, high], axis=0)], axis=1
    )
    for g in range(NX):
        share = LAT // NX
        turned = whole if g == 0 else pltpu.roll(whole, WIDE - share * g, axis=1)
        quarters[g] = turned[:, :share].astype(BF16)
    for d, peer in enumerate(far):
        copy = pltpu.make_async_remote_copy(
            src_ref=quarters.at[peer[1]],
            dst_ref=lat_out.at[x],
            send_sem=lsend.at[d],
            recv_sem=lrecv.at[d],
            device_id=peer,
            device_id_type=MESH,
        )
        copy.start()
        sends.append(copy)
    lat_out[x] = quarters[x]

    for number_here in range(7):
        pltpu.make_async_copy(
            dq_got.at[number_here], dq_got.at[number_here], qrecv.at[number_here]
        ).wait()
    for pair in range(HEADS_HERE // 2):
        rows = pl.ds(16 * pair, 16)
        value = dq_ref[core, x, rows, :].astype(F32)
        for number_here in range(7):
            value = value + dq_got[number_here, rows, :].astype(F32)
        one, two = value[:QBLK], pltpu.roll(value[QBLK:], 64, axis=1)
        dq_out[:, 2 * LAT * pair : 2 * LAT * (pair + 1)] = jnp.concatenate(
            [one[:, :VDIM], one[:, VDIM:] + two[:, :128], two[:, 128:]], axis=1
        ).astype(BF16)
    for d in range(3):
        pltpu.make_async_copy(lat_out.at[0], lat_out.at[0], lrecv.at[d]).wait()
    for copy in sends:
        copy.wait_send()


def return_all(dkeys, dq):
    vmem = pl.BlockSpec(memory_space=pltpu.VMEM)
    return pl.pallas_call(
        return_kernel,
        out_shape=(
            jax.ShapeDtypeStruct((QBLK, HEADS_HERE * LAT), BF16),
            jax.ShapeDtypeStruct((4, BLK, LAT // NX), BF16),
        ),
        in_specs=[vmem, vmem],
        out_specs=(vmem, vmem),
        scratch_shapes=[
            pltpu.VMEM((2 * NLAB, HALF, 128), BF16),
            pltpu.VMEM((2, len(OFFS), HALF, 128), BF16),
            pltpu.VMEM((ROWS, 128), F32),
            pltpu.VMEM((NX, BLK, LAT // NX), BF16),
            pltpu.VMEM((7, QR, WIDE), BF16),
            pltpu.SemaphoreType.DMA((2 * NLAB,)),
            pltpu.SemaphoreType.DMA((2 * NLAB,)),
            pltpu.SemaphoreType.DMA((7,)),
            pltpu.SemaphoreType.DMA((7,)),
            pltpu.SemaphoreType.DMA((3,)),
            pltpu.SemaphoreType.DMA((3,)),
        ],
        compiler_params=pltpu.CompilerParams(
            collective_id=2, has_side_effects=True, vmem_limit_bytes=VMEM_LIMIT
        ),
        cost_estimate=pl.CostEstimate(flops=0, bytes_accessed=10_000_000, transcendentals=0),
        name="return_grads",
    )(dkeys, dq)


def local(queries, grad_out, latent, selected):
    keys, all_q, all_g, sel, stats = gather_all(latent, queries, grad_out, selected)
    all_q = all_q.reshape(NK, ALLR, WIDE)
    all_g = all_g.reshape(NK, ALLR, VDIM)
    dkeys, dq = grads_of(sel, keys, all_q, all_g, stats)
    return return_all(dkeys, dq)


def solution(mesh):
    placed = (P("ctx", "head"), P("ctx", "head"), P("ctx", None, None), P("ctx", None))
    return jax.shard_map(
        local,
        mesh=mesh,
        in_specs=placed,
        out_specs=(P("ctx", "head"), P("ctx", None, "head")),
        check_vma=False,
    )
```

```python
import functools

import jax
import jax.numpy as jnp
from jax import lax
from jax.experimental import pallas as pl
from jax.experimental.pallas import tpu as pltpu
from jax.sharding import PartitionSpec as P

MESH = pl.DeviceIdType.MESH
BF16 = jnp.bfloat16
F32 = jnp.float32
SCALE = 192.0 ** (-0.5)

NY, NZ, NK, NX = 8, 8, 2, 4
RING = 8
BLK, LAT, VDIM = 64, 576, 512
WIDE = 640
ROWS = 288
HALF = 144
QBLK, HEADS_HERE = 8, 16
QR = QBLK * HEADS_HERE
ALLR = QR * NX
SLOTS = 32
CHUNK = 4
GROUP = 4
CK = CHUNK * BLK
NEG = -1e30
VMEM_LIMIT = 24 * 1024 * 1024

OFFS = (0, -1, 1, -2, 2, -3, 3, -4)
UP = (4, 4, 4, 4, 3, 3, 3, 3)
DOWN = (3, 3, 3, 3, 4, 4, 4, 4)


def where_am_i():
    ctx = lax.axis_index("ctx")
    x = lax.axis_index("head")
    core = lax.rem(ctx, NK)
    chip = ctx // NK
    return lax.rem(chip, NZ), chip // NZ, core, x


def ctx_of(y, z, core):
    return (y * NZ + z) * NK + core


def wrap(v, n):
    return lax.rem(v + 2 * n, n)


def place(half, first, second):
    return second * NZ + first if half == 0 else first * NZ + second


def neighbour(half, ring, step, y, z, core, x):
    along_z = (half == 0) == (ring == 0)
    if along_z:
        return (ctx_of(y, wrap(z + step, NZ), core), x)
    return (ctx_of(wrap(y + step, NY), z, core), x)


READY, WORK = 15.0, 0.5
PASS = ((6.0, (0, 3)), (6.2, (1, 1)), (9.0, (1, 3)), (9.2, (0, 1)), (12.0, (0, 2)), (12.2, (1, 2)))
PIECE, DELAY = 0.72, 1.5


def gather_plan():
    sends = {}
    for half in (0, 1):
        for t in range(4):
            sends[(half, 0, 1, t, 0)] = (half, 0, 1, t - 1, 0) if t else None
        for t in range(3):
            sends[(half, 0, -1, t, 0)] = (half, 0, -1, t - 1, 0) if t else None
        for q, off in enumerate(OFFS):
            root = (half, 0, 1 if off < 0 else -1, abs(off) - 1, 0) if off else None
            for s in range(UP[q]):
                sends[(half, 1, 1, s, q)] = (half, 1, 1, s - 1, q) if s else root
            for s in range(DOWN[q]):
                sends[(half, 1, -1, s, q)] = (half, 1, -1, s - 1, q) if s else root
    left = {}
    for key in sends:
        length, at = 0, key
        while at is not None:
            left[at] = max(left.get(at, 0), length)
            length, at = length + 1, sends[at]
    free, ready, order = {}, {k: 0.0 for k in sends if sends[k] is None}, []

    def link(key):
        return (key[0] ^ key[1], key[2])

    while ready:
        at = min(ready, key=lambda k: (round(max(ready[k], free.get(link(k), 0.0)), 3), -left[k], k))
        since = ready.pop(at)
        begin = max(since, free.get(link(at), 0.0))
        free[link(at)] = begin + PIECE
        order.append((begin, since, at))
        for key, root in sends.items():
            if root == at:
                ready[key] = begin + PIECE + DELAY
    return order


def labels():
    names = {}
    for begin, since, (half, ring, way, s, q) in gather_plan():
        if half == 0:
            names[(ring, way, s + 1, q)] = len(names)
    return names


LABELS = labels()


def route(half, dy, dz):
    off, along = (dz, dy) if half == 0 else (dy, dz)
    if along == 0:
        return None if off == 0 else (0, 1 if off < 0 else -1, abs(off), 0)
    q = OFFS.index(off)
    if along == -4 and UP[q] < 4:
        return (1, -1, 4, q)
    return (1, 1 if along < 0 else -1, abs(along), q)


def gather_steps():
    lands = {(None, 0): 0.0, (None, 1): 0.0}
    for begin, since, (half, ring, way, s, q) in gather_plan():
        lands[((ring, way, s + 1, q), half)] = begin + PIECE + DELAY
    blocks = []
    for dy in OFFS:
        for dz in OFFS:
            blocks.append((max(lands[(route(half, dy, dz), half)] for half in (0, 1)), dy, dz))
    blocks.sort(key=lambda b: (b[0], abs(b[1]) + abs(b[2]), b))
    work, clock = [], READY
    for first in range(0, len(blocks), GROUP):
        group = blocks[first : first + GROUP]
        clock = max(clock, group[-1][0] * 1.15 + 0.5)
        work.append((clock, [b[1:] for b in group]))
        clock = clock + 2 * WORK
    sends = gather_plan()
    merged = []
    marks = [(1.0, "start")] + [(t, "pass") + what for t, what in PASS] + [(t, "work", group) for t, group in work]
    marks.sort(key=lambda m: m[0])
    for mark in marks:
        for entry in [e for e in sends if e[1] * 1.15 + 0.5 <= mark[0] or mark[1] in ('start', 'pass') and e[1] <= mark[0]]:
            merged.append(("send", entry[2]))
            sends.remove(entry)
        merged.append(mark[1:])
    return merged + [("send", entry[2]) for entry in sends]
NLAB = len(LABELS)


def enter(peers):
    barrier = pltpu.get_barrier_semaphore()
    for peer in peers:
        pl.semaphore_signal(barrier, inc=1, device_id=peer, device_id_type=MESH)
    pl.semaphore_wait(barrier, len(peers))


def ring_peers(y, z, core, x):
    return [neighbour(0, ring, step, y, z, core, x) for ring in (0, 1) for step in (1, -1)]


def group_peers(y, z, core, x):
    me = ctx_of(y, z, core)
    sibling = ctx_of(y, z, 1 - core)
    far = [(me, wrap(x + d, NX)) for d in (1, 2, 3)]
    across = [(sibling, wrap(x + d, NX)) for d in (0, 1, 2, 3)]
    return far, across


def pack_block(block):
    parts = [block[:, 128 * g : 128 * g + 128] for g in range(4)]
    return parts, block[:, VDIM:]


def gather_kernel(
    lat_ref, q_hbm, g_hbm, sel_ref,
    keys_out, q_out, g_out, sel_out, stats_all,
    block, pack, q_ref, g_ref, qrow, grow, stats, unseen,
    load_sem, local_sem, send_sem, recv_sem, gsend, grecv, ssend, srecv,
):
    z, y, core, x = where_am_i()
    chip = y * NZ + z
    load = pltpu.make_async_copy(lat_ref.at[x], block, load_sem)
    load.start()
    load_q = pltpu.make_async_copy(q_hbm, q_ref, local_sem.at[4])
    load_q.start()
    load_g = pltpu.make_async_copy(g_hbm, g_ref, local_sem.at[5])
    load_g.start()
    far, across = group_peers(y, z, core, x)
    enter(ring_peers(y, z, core, x) + far + across)
    load.wait()
    wide = block[...].astype(F32)
    for g in range(4):
        pack[64 * g : 64 * g + 64, :] = block[:, 128 * g : 128 * g + 128]
    tail = jnp.concatenate([wide[:, VDIM:], jnp.zeros((BLK, 64), F32)], axis=1)
    pack[256:288, :] = (tail[:32] + pltpu.roll(tail[32:], 64, axis=1)).astype(BF16)
    keep = pltpu.make_async_copy(pack, keys_out.at[chip], local_sem.at[0])
    keep.start()

    first = {0: z, 1: y}
    second = {0: y, 1: z}
    sends = []
    arrived = set()

    def part(half):
        return pl.ds(HALF * half, HALF)

    def arrival(half, label):
        if (half, label) in arrived:
            return
        arrived.add((half, label))
        pltpu.make_async_copy(
            keys_out.at[chip, part(half)], keys_out.at[chip, part(half)],
            recv_sem.at[half * NLAB + LABELS[label]],
        ).wait()

    def send(half, ring, way, s, q):
        if ring == 0:
            off, along = -way * s, 0
            if s > 0:
                arrival(half, (0, way, s, 0))
        else:
            off, along = OFFS[q], -way * s
            if s > 0:
                arrival(half, (1, way, s, q))
            elif off != 0:
                arrival(half, (0, 1 if off < 0 else -1, abs(off), 0))
        spot = place(half, wrap(first[half] + off, RING), wrap(second[half] + along, RING))
        own = off == 0 and along == 0
        src = pack.at[part(half)] if own else keys_out.at[spot, part(half)]
        number = half * NLAB + LABELS[(ring, way, s + 1, q)]
        copy = pltpu.make_async_remote_copy(
            src_ref=src,
            dst_ref=keys_out.at[spot, part(half)],
            send_sem=send_sem.at[number],
            recv_sem=recv_sem.at[number],
            device_id=neighbour(half, ring, way, y, z, core, x),
            device_id_type=MESH,
        )
        copy.start()
        sends.append(copy)

    def group_copy(src, out, kind, slot_core, slot_x, peer, number):
        copy = pltpu.make_async_remote_copy(
            src_ref=src,
            dst_ref=out.at[slot_core, slot_x] if kind != 2 else out.at[slot_core],
            send_sem=gsend.at[number],
            recv_sem=grecv.at[number],
            device_id=peer,
            device_id_type=MESH,
        )
        copy.start()
        sends.append(copy)

    group_number = {}

    def number_of(kind, hop):
        return group_number.setdefault((kind, hop), len(group_number))

    def group_arrival(kind, hop):
        ref = (q_out.at[0, 0], g_out.at[0, 0], sel_out.at[0])[kind]
        pltpu.make_async_copy(ref, ref, grecv.at[number_of(kind, hop)]).wait()

    def start_group():
        group_copy(sel_ref, sel_out, 2, core, 0, across[0], number_of(2, 0))
        keep_sel.start()
        load_q.wait()
        load_g.wait()
        for pair in range(HEADS_HERE // 2):
            both = q_ref[:, 2 * LAT * pair : 2 * LAT * (pair + 1)].astype(F32)
            lane = lax.broadcasted_iota(jnp.int32, (QBLK, WIDE), 1)
            one = jnp.where(lane < LAT, both[:, :WIDE], 0.0)
            two = jnp.where(lane < LAT, pltpu.roll(both[:, VDIM:], WIDE - 64, axis=1), 0.0)
            qrow[16 * pair : 16 * pair + 16, :] = jnp.concatenate([one, two], axis=0).astype(BF16)
            one = g_ref[:, 2 * VDIM * pair : 2 * VDIM * pair + VDIM].astype(F32)
            two = g_ref[:, 2 * VDIM * pair + VDIM : 2 * VDIM * (pair + 1)].astype(F32)
            grow[16 * pair : 16 * pair + 16, :] = jnp.concatenate([one, two], axis=0).astype(BF16)
        group_copy(qrow, q_out, 0, core, x, far[0], number_of(0, 3))
        group_copy(grow, g_out, 1, core, x, far[2], number_of(1, 1))
        group_copy(qrow, q_out, 0, core, x, across[0], number_of(0, 4))
        group_copy(grow, g_out, 1, core, x, across[0], number_of(1, 4))
        group_copy(grow, g_out, 1, core, x, far[0], number_of(1, 3))
        group_copy(qrow, q_out, 0, core, x, far[2], number_of(0, 1))
        keep_q.start()
        keep_g.start()

    def pass_on(kind, hop):
        src_x = wrap(x + hop, NX)
        group_arrival(kind, hop)
        out = (q_out, g_out)[kind]
        if (kind, hop) == (0, 3):
            group_copy(out.at[core, src_x], out, kind, core, src_x, far[0], number_of(kind, 2))
        if (kind, hop) == (1, 1):
            group_copy(out.at[core, src_x], out, kind, core, src_x, far[2], number_of(kind, 2))
        group_copy(out.at[core, src_x], out, kind, core, src_x, across[0], number_of(kind, 4 + hop))

    keep_sel = pltpu.make_async_copy(sel_ref, sel_out.at[core], local_sem.at[1])
    keep_q = pltpu.make_async_copy(qrow, q_out.at[core, x], local_sem.at[2])
    keep_g = pltpu.make_async_copy(grow, g_out.at[core, x], local_sem.at[3])
    def group_done():
        for kind in (0, 1):
            for hop in (4, 5, 6, 7):
                group_arrival(kind, hop)
        group_arrival(2, 0)
        keep_sel.wait()
        keep_q.wait()
        keep_g.wait()
        ids = lax.broadcasted_iota(jnp.int32, (NY * NZ, SLOTS), 0) * 8 + 4 * core + x
        for qb in range(NK):
            hit = jnp.max(jnp.where(sel_out[qb] == ids, 1.0, 0.0), axis=1, keepdims=True)
            unseen[qb] = jnp.broadcast_to(jnp.where(hit > 0.0, 0.0, NEG), (NY * NZ, 128))
            stats[3 * qb : 3 * qb + 3, :] = jnp.concatenate(
                [jnp.full((1, ALLR), NEG, F32), jnp.zeros((2, ALLR), F32)], axis=0
            )

    lane = lax.broadcasted_iota(jnp.int32, (32, 128), 1)

    def work(group):
        fronts, tails, hides = [], [], [[], []]
        for dy, dz in group:
            for half in (0, 1):
                label = route(half, dy, dz)
                if label is not None:
                    arrival(half, label)
            spot = wrap(y + dy, NY) * NZ + wrap(z + dz, NZ)
            if (dy, dz) == (0, 0):
                keep.wait()
            fronts.append(jnp.concatenate([keys_out[spot, 64 * g : 64 * g + 64, :] for g in range(4)], axis=1))
            tail = keys_out[spot, 256:288, :].astype(F32)
            low = jnp.where(lane < 64, tail, 0.0)
            high = jnp.where(lane < 64, pltpu.roll(tail, 64, axis=1), 0.0)
            tails.append(jnp.concatenate([low, high], axis=0).astype(BF16))
            for qb in range(NK):
                hide = jnp.concatenate([unseen[qb, pl.ds(spot, 1), :]] * 4, axis=1)
                hide = jnp.broadcast_to(hide, (BLK, ALLR))
                if (dy, dz) == (0, 0):
                    row = lax.broadcasted_iota(jnp.int32, (BLK, ALLR), 0)
                    col = lax.broadcasted_iota(jnp.int32, (BLK, ALLR), 1)
                    late = row > BLK - QBLK + lax.rem(col, QBLK)
                    own = (x == NX - 1) & (core == qb)
                    hide = jnp.where(late & own, NEG, hide)
                hides[qb].append(hide)
        front = jnp.concatenate(fronts, axis=0)
        whole = jnp.concatenate([front, jnp.concatenate(tails, axis=0)], axis=1)
        scores = [nt(whole, q_out[qb].reshape(ALLR, WIDE)) for qb in range(NK)]
        dprobs = [nt(front, g_out[qb].reshape(ALLR, VDIM)) for qb in range(NK)]
        for qb in range(NK):
            score = SCALE * scores[qb] + jnp.concatenate(hides[qb], axis=0)
            top = stats[3 * qb : 3 * qb + 1, :]
            new_top = jnp.maximum(top, jnp.max(score, axis=0, keepdims=True))
            weights = jnp.exp(score - new_top)
            shrink = jnp.exp(top - new_top)
            total = stats[3 * qb + 1 : 3 * qb + 2, :] * shrink + jnp.sum(weights, axis=0, keepdims=True)
            delta = stats[3 * qb + 2 : 3 * qb + 3, :] * shrink + jnp.sum(weights * dprobs[qb], axis=0, keepdims=True)
            stats[3 * qb : 3 * qb + 3, :] = jnp.concatenate([new_top, total, delta], axis=0)

    stats[...] = jnp.zeros((8, ALLR), F32)
    begun = False
    for mark in gather_steps():
        if mark[0] == "send":
            send(*mark[1])
        elif mark[0] == "start":
            start_group()
        elif mark[0] == "pass":
            pass_on(*mark[1:])
        else:
            if not begun:
                group_done()
                begun = True
            work(*mark[1:])

    slot = x * NK + core
    for number, peer in enumerate(far + across):
        copy = pltpu.make_async_remote_copy(
            src_ref=stats,
            dst_ref=stats_all.at[slot],
            send_sem=ssend.at[number],
            recv_sem=srecv.at[number],
            device_id=peer,
            device_id_type=MESH,
        )
        copy.start()
        sends.append(copy)
    stats_all[slot] = stats[...]
    for number in range(7):
        pltpu.make_async_copy(stats_all.at[0], stats_all.at[0], srecv.at[number]).wait()
    for copy in sends:
        copy.wait_send()


def gather_all(latent, queries, grad_out, selected):
    hbm = pl.BlockSpec(memory_space=pltpu.HBM)
    vmem = pl.BlockSpec(memory_space=pltpu.VMEM)
    return pl.pallas_call(
        gather_kernel,
        out_shape=(
            jax.ShapeDtypeStruct((NY * NZ, ROWS, 128), BF16),
            jax.ShapeDtypeStruct((NK, NX, QR, WIDE), BF16),
            jax.ShapeDtypeStruct((NK, NX, QR, VDIM), BF16),
            jax.ShapeDtypeStruct((NK, 1, SLOTS), jnp.int32),
            jax.ShapeDtypeStruct((NX * NK, 8, ALLR), F32),
        ),
        in_specs=[hbm] * 4,
        out_specs=(vmem,) * 5,
        scratch_shapes=[
            pltpu.VMEM((BLK, LAT), BF16),
            pltpu.VMEM((ROWS, 128), BF16),
            pltpu.VMEM((QBLK, HEADS_HERE * LAT), BF16),
            pltpu.VMEM((QBLK, HEADS_HERE * VDIM), BF16),
            pltpu.VMEM((QR, WIDE), BF16),
            pltpu.VMEM((QR, VDIM), BF16),
            pltpu.VMEM((8, ALLR), F32),
            pltpu.VMEM((NK, NY * NZ, 128), F32),
            pltpu.SemaphoreType.DMA(()),
            pltpu.SemaphoreType.DMA((6,)),
            pltpu.SemaphoreType.DMA((2 * NLAB,)),
            pltpu.SemaphoreType.DMA((2 * NLAB,)),
            pltpu.SemaphoreType.DMA((15,)),
            pltpu.SemaphoreType.DMA((15,)),
            pltpu.SemaphoreType.DMA((7,)),
            pltpu.SemaphoreType.DMA((7,)),
        ],
        compiler_params=pltpu.CompilerParams(
            collective_id=0, has_side_effects=True, vmem_limit_bytes=VMEM_LIMIT
        ),
        cost_estimate=pl.CostEstimate(flops=0, bytes_accessed=10_000_000, transcendentals=0),
        name="gather_keys",
    )(*[pltpu.with_memory_space_constraint(a, pltpu.HBM) for a in (latent, queries, grad_out, selected)])


def list_slots(sel_ref, spots, owns, query_block, kind, own_id):
    def look(j, n):
        block_id = sel_ref[query_block, 0, j]
        mine = (block_id >= 0) & (lax.rem(block_id, 8) == kind)
        spots[n] = jnp.where(mine, block_id // 8, 0)
        owns[n] = jnp.where(mine & (block_id == own_id), 1, 0)
        return n + mine.astype(jnp.int32)

    count = lax.fori_loop(0, SLOTS, look, jnp.int32(0))
    for extra in range(CHUNK):
        spots[count + extra] = 0
        owns[count + extra] = 0
    return count


def take_chunk(chunk, spots, keys_ref, kbuf):
    lane = lax.broadcasted_iota(jnp.int32, (32, 128), 1)
    for i in range(CHUNK):
        spot = spots[chunk * CHUNK + i]
        for g in range(4):
            kbuf[64 * i : 64 * i + 64, 128 * g : 128 * g + 128] = keys_ref[spot, 64 * g : 64 * g + 64, :]
        tail = keys_ref[spot, 256:288, :].astype(F32)
        kbuf[64 * i : 64 * i + 32, VDIM:] = jnp.where(lane < 64, tail, 0.0).astype(BF16)
        kbuf[64 * i + 32 : 64 * i + 64, VDIM:] = jnp.where(
            lane < 64, pltpu.roll(tail, 64, axis=1), 0.0
        ).astype(BF16)


def seen_of(chunk, owns, count):
    row = lax.broadcasted_iota(jnp.int32, (BLK, ALLR), 0)
    col = lax.broadcasted_iota(jnp.int32, (BLK, ALLR), 1)
    limit = BLK - QBLK + lax.rem(col, QBLK)
    parts = []
    for i in range(CHUNK):
        slot = chunk * CHUNK + i
        top = jnp.where(slot < count, jnp.where(owns[slot] == 1, limit, BLK), -1)
        parts.append(row <= top)
    return jnp.concatenate(parts, axis=0)


def nt(a, b):
    return lax.dot_general(a, b, (((1,), (1,)), ((), ())), preferred_element_type=F32)


def tn(a, b):
    return lax.dot_general(a, b, (((0,), (0,)), ((), ())), preferred_element_type=F32)


def nn(a, b):
    return lax.dot_general(a, b, (((1,), (0,)), ((), ())), preferred_element_type=F32)


def grads_kernel(
    sel_ref, keys_ref, q_ref, g_ref, stats_ref, dkeys_ref, dq_ref, kbuf, dq_acc, spots, owns
):
    z, y, core, x = where_am_i()
    chip = y * NZ + z

    def clear(i, carry):
        dkeys_ref[i] = jnp.zeros((ROWS, 128), BF16)
        return carry

    lax.fori_loop(0, NY * NZ, clear, 0)
    for qb in range(NK):
        count = list_slots(sel_ref, spots, owns, qb, 4 * core + x, (chip * NK + qb) * 4 + 3)
        chunks = (count + CHUNK - 1) // CHUNK

        top = stats_ref[0, 3 * qb : 3 * qb + 1, :]
        for d in range(1, NX * NK):
            top = jnp.maximum(top, stats_ref[d, 3 * qb : 3 * qb + 1, :])
        total = jnp.zeros((1, ALLR), F32)
        delta = jnp.zeros((1, ALLR), F32)
        for d in range(NX * NK):
            shrink = jnp.exp(stats_ref[d, 3 * qb : 3 * qb + 1, :] - top)
            total = total + shrink * stats_ref[d, 3 * qb + 1 : 3 * qb + 2, :]
            delta = delta + shrink * stats_ref[d, 3 * qb + 2 : 3 * qb + 3, :]
        inverse = 1.0 / total
        delta = delta * inverse
        dq_acc[...] = jnp.zeros((ALLR, WIDE), F32)

        def step(chunk, carry):
            take_chunk(chunk, spots, keys_ref, kbuf)
            seen = seen_of(chunk, owns, count)
            scores = SCALE * nt(kbuf[...], q_ref[qb])
            dprobs = nt(kbuf[:, :VDIM], g_ref[qb])
            probs = jnp.where(seen, jnp.exp(jnp.where(seen, scores, NEG) - top), 0.0) * inverse
            probs16 = probs.astype(BF16)
            dscores16 = (probs * (dprobs - delta)).astype(BF16)
            dq_acc[...] += tn(dscores16, kbuf[...])
            dkeys = SCALE * nn(dscores16, q_ref[qb])
            dvalues = nn(probs16, g_ref[qb])
            front = dkeys[:, :VDIM] + dvalues
            back = dkeys[:, VDIM:]
            for i in range(CHUNK):
                slot_now = chunk * CHUNK + i

                @pl.when(slot_now < count)
                def _():
                    spot = spots[slot_now]
                    for g in range(4):
                        old = dkeys_ref[spot, 64 * g : 64 * g + 64, :].astype(F32)
                        new = front[64 * i : 64 * i + 64, 128 * g : 128 * g + 128]
                        dkeys_ref[spot, 64 * g : 64 * g + 64, :] = (old + new).astype(BF16)
                    old = dkeys_ref[spot, 256:288, :].astype(F32)
                    new = back[64 * i : 64 * i + 32] + pltpu.roll(back[64 * i + 32 : 64 * i + 64], 64, axis=1)
                    dkeys_ref[spot, 256:288, :] = (old + new).astype(BF16)

            return carry

        lax.fori_loop(0, chunks, step, 0)
        for g in range(NX):
            dq_ref[qb, g] = (SCALE * dq_acc[QR * g : QR * g + QR, :]).astype(BF16)


def grads_of(sel, keys, queries, grad_out, stats):
    vmem = pl.BlockSpec(memory_space=pltpu.VMEM)
    return pl.pallas_call(
        grads_kernel,
        out_shape=(
            jax.ShapeDtypeStruct((NY * NZ, ROWS, 128), BF16),
            jax.ShapeDtypeStruct((NK, NX, QR, WIDE), BF16),
        ),
        in_specs=[
            pl.BlockSpec(memory_space=pltpu.SMEM),
            vmem,
            vmem,
            vmem,
            vmem,
        ],
        out_specs=(vmem, vmem),
        scratch_shapes=[
            pltpu.VMEM((CK, WIDE), BF16),
            pltpu.VMEM((ALLR, WIDE), F32),
            pltpu.SMEM((SLOTS + CHUNK,), jnp.int32),
            pltpu.SMEM((SLOTS + CHUNK,), jnp.int32),
        ],
        compiler_params=pltpu.CompilerParams(vmem_limit_bytes=VMEM_LIMIT),
        name="local_grads",
    )(sel, keys, queries, grad_out, stats)


def return_kernel(
    dkeys_ref, dq_ref, dq_out, lat_out,
    got, tsum, total, quarters, dq_got, send_sem, recv_sem, qsend, qrecv, lsend, lrecv,
):
    z, y, core, x = where_am_i()
    far, across = group_peers(y, z, core, x)
    peers = far + across
    enter(ring_peers(y, z, core, x) + peers)
    first = {0: z, 1: y}
    second = {0: y, 1: z}
    sends = []

    def part(half):
        return pl.ds(HALF * half, HALF)

    def number(half, ring, way, left, q):
        return half * NLAB + LABELS[(ring, -way, left + 1, q)]

    def arrival(half, ring, way, left, q):
        at = number(half, ring, way, left, q)
        pltpu.make_async_copy(got.at[at], got.at[at], recv_sem.at[at]).wait()
        return at

    def local(half, off, along):
        spot = place(half, wrap(first[half] + off, RING), wrap(second[half] + along, RING))
        return dkeys_ref.at[spot, part(half)]

    def push(src, half, ring, way, left, q):
        at = number(half, ring, way, left, q)
        copy = pltpu.make_async_remote_copy(
            src_ref=src,
            dst_ref=got.at[at],
            send_sem=send_sem.at[at],
            recv_sem=recv_sem.at[at],
            device_id=neighbour(half, ring, way, y, z, core, x),
            device_id_type=MESH,
        )
        copy.start()
        sends.append(copy)

    def row_total(half, q):
        value = local(half, OFFS[q], 0)[...].astype(F32)
        for way in (1, -1):
            at = arrival(half, 1, way, 0, q)
            value = value + got[at].astype(F32)
        return value

    def send_row(half, q):
        off = OFFS[q]
        way, dist = (1, off) if off > 0 else (-1, -off)
        value = row_total(half, q)
        if (0, -way, dist + 1, 0) in LABELS:
            at = arrival(half, 0, way, dist, 0)
            value = value + got[at].astype(F32)
        tsum[half, q] = value.astype(BF16)
        push(tsum.at[half, q], half, 0, way, dist - 1, 0)

    def send_big(half, way, left, q):
        reach = UP[q] if way == -1 else DOWN[q]
        if left == reach - 1:
            push(local(half, OFFS[q], way * (left + 1)), half, 1, way, left, q)
        else:
            at = arrival(half, 1, way, left + 1, q)
            got[at] = (got[at].astype(F32) + local(half, OFFS[q], way * (left + 1))[...].astype(F32)).astype(BF16)
            push(got.at[at], half, 1, way, left, q)

    for turn, (begin, since, (half, ring, way, s, q)) in enumerate(reversed(gather_plan())):
        if ring == 0:
            send_row(half, OFFS.index(-way * (s + 1)))
        else:
            send_big(half, -way, s, q)
        if turn == 24:
            for number_here, (ctx, head) in enumerate(peers):
                to_core = core if number_here < 3 else 1 - core
                copy = pltpu.make_async_remote_copy(
                    src_ref=dq_ref.at[to_core, head],
                    dst_ref=dq_got.at[number_here],
                    send_sem=qsend.at[number_here],
                    recv_sem=qrecv.at[number_here],
                    device_id=(ctx, head),
                    device_id_type=MESH,
                )
                copy.start()
                sends.append(copy)

    for half in (0, 1):
        value = row_total(half, 0)
        for way in (1, -1):
            at = arrival(half, 0, way, 0, 0)
            value = value + got[at].astype(F32)
        total[HALF * half : HALF * half + HALF, :] = value

    lane = lax.broadcasted_iota(jnp.int32, (32, 128), 1)
    tail = total[256:288, :]
    low = jnp.where(lane < 64, tail, 0.0)
    high = jnp.where(lane < 64, pltpu.roll(tail, 64, axis=1), 0.0)
    whole = jnp.concatenate(
        [total[64 * g : 64 * g + 64, :] for g in range(4)] + [jnp.concatenate([low, high], axis=0)], axis=1
    )
    for g in range(NX):
        share = LAT // NX
        turned = whole if g == 0 else pltpu.roll(whole, WIDE - share * g, axis=1)
        quarters[g] = turned[:, :share].astype(BF16)
    for d, peer in enumerate(far):
        copy = pltpu.make_async_remote_copy(
            src_ref=quarters.at[peer[1]],
            dst_ref=lat_out.at[x],
            send_sem=lsend.at[d],
            recv_sem=lrecv.at[d],
            device_id=peer,
            device_id_type=MESH,
        )
        copy.start()
        sends.append(copy)
    lat_out[x] = quarters[x]

    for number_here in range(7):
        pltpu.make_async_copy(
            dq_got.at[number_here], dq_got.at[number_here], qrecv.at[number_here]
        ).wait()
    for pair in range(HEADS_HERE // 2):
        rows = pl.ds(16 * pair, 16)
        value = dq_ref[core, x, rows, :].astype(F32)
        for number_here in range(7):
            value = value + dq_got[number_here, rows, :].astype(F32)
        one, two = value[:QBLK], pltpu.roll(value[QBLK:], 64, axis=1)
        dq_out[:, 2 * LAT * pair : 2 * LAT * (pair + 1)] = jnp.concatenate(
            [one[:, :VDIM], one[:, VDIM:] + two[:, :128], two[:, 128:]], axis=1
        ).astype(BF16)
    for d in range(3):
        pltpu.make_async_copy(lat_out.at[0], lat_out.at[0], lrecv.at[d]).wait()
    for copy in sends:
        copy.wait_send()


def return_all(dkeys, dq):
    vmem = pl.BlockSpec(memory_space=pltpu.VMEM)
    return pl.pallas_call(
        return_kernel,
        out_shape=(
            jax.ShapeDtypeStruct((QBLK, HEADS_HERE * LAT), BF16),
            jax.ShapeDtypeStruct((4, BLK, LAT // NX), BF16),
        ),
        in_specs=[vmem, vmem],
        out_specs=(vmem, vmem),
        scratch_shapes=[
            pltpu.VMEM((2 * NLAB, HALF, 128), BF16),
            pltpu.VMEM((2, len(OFFS), HALF, 128), BF16),
            pltpu.VMEM((ROWS, 128), F32),
            pltpu.VMEM((NX, BLK, LAT // NX), BF16),
            pltpu.VMEM((7, QR, WIDE), BF16),
            pltpu.SemaphoreType.DMA((2 * NLAB,)),
            pltpu.SemaphoreType.DMA((2 * NLAB,)),
            pltpu.SemaphoreType.DMA((7,)),
            pltpu.SemaphoreType.DMA((7,)),
            pltpu.SemaphoreType.DMA((3,)),
            pltpu.SemaphoreType.DMA((3,)),
        ],
        compiler_params=pltpu.CompilerParams(
            collective_id=2, has_side_effects=True, vmem_limit_bytes=VMEM_LIMIT
        ),
        cost_estimate=pl.CostEstimate(flops=0, bytes_accessed=10_000_000, transcendentals=0),
        name="return_grads",
    )(dkeys, dq)


def local(queries, grad_out, latent, selected):
    keys, all_q, all_g, sel, stats = gather_all(latent, queries, grad_out, selected)
    all_q = all_q.reshape(NK, ALLR, WIDE)
    all_g = all_g.reshape(NK, ALLR, VDIM)
    dkeys, dq = grads_of(sel, keys, all_q, all_g, stats)
    return return_all(dkeys, dq)


def solution(mesh):
    placed = (P("ctx", "head"), P("ctx", "head"), P("ctx", None, None), P("ctx", None))
    return jax.shard_map(
        local,
        mesh=mesh,
        in_specs=placed,
        out_specs=(P("ctx", "head"), P("ctx", None, "head")),
        check_vma=False,
    )
```

```python
import functools

import jax
import jax.numpy as jnp
from jax import lax
from jax.experimental import pallas as pl
from jax.experimental.pallas import tpu as pltpu
from jax.sharding import PartitionSpec as P

MESH = pl.DeviceIdType.MESH
BF16 = jnp.bfloat16
F32 = jnp.float32
SCALE = 192.0 ** (-0.5)

NY, NZ, NK, NX = 8, 8, 2, 4
RING = 8
BLK, LAT, VDIM = 64, 576, 512
WIDE = 640
ROWS = 288
HALF = 144
QBLK, HEADS_HERE = 8, 16
QR = QBLK * HEADS_HERE
ALLR = QR * NX
SLOTS = 32
CHUNK = 4
GROUP = 4
CK = CHUNK * BLK
NEG = -1e30
VMEM_LIMIT = 24 * 1024 * 1024

OFFS = (0, -1, 1, -2, 2, -3, 3, -4)
UP = (4, 4, 4, 4, 3, 3, 3, 3)
DOWN = (3, 3, 3, 3, 4, 4, 4, 4)


def where_am_i():
    ctx = lax.axis_index("ctx")
    x = lax.axis_index("head")
    core = lax.rem(ctx, NK)
    chip = ctx // NK
    return lax.rem(chip, NZ), chip // NZ, core, x


def ctx_of(y, z, core):
    return (y * NZ + z) * NK + core


def wrap(v, n):
    return lax.rem(v + 2 * n, n)


def place(half, first, second):
    return second * NZ + first if half == 0 else first * NZ + second


def neighbour(half, ring, step, y, z, core, x):
    along_z = (half == 0) == (ring == 0)
    if along_z:
        return (ctx_of(y, wrap(z + step, NZ), core), x)
    return (ctx_of(wrap(y + step, NY), z, core), x)


READY, WORK = 14.0, 0.5
PASS = ((6.0, (0, 3)), (6.2, (1, 1)), (9.0, (1, 3)), (9.2, (0, 1)), (12.0, (0, 2)), (12.2, (1, 2)))
PIECE, DELAY = 0.72, 1.5


def gather_plan():
    sends = {}
    for half in (0, 1):
        for t in range(4):
            sends[(half, 0, 1, t, 0)] = (half, 0, 1, t - 1, 0) if t else None
        for t in range(3):
            sends[(half, 0, -1, t, 0)] = (half, 0, -1, t - 1, 0) if t else None
        for q, off in enumerate(OFFS):
            root = (half, 0, 1 if off < 0 else -1, abs(off) - 1, 0) if off else None
            for s in range(UP[q]):
                sends[(half, 1, 1, s, q)] = (half, 1, 1, s - 1, q) if s else root
            for s in range(DOWN[q]):
                sends[(half, 1, -1, s, q)] = (half, 1, -1, s - 1, q) if s else root
    left = {}
    for key in sends:
        length, at = 0, key
        while at is not None:
            left[at] = max(left.get(at, 0), length)
            length, at = length + 1, sends[at]
    free, ready, order = {}, {k: 0.0 for k in sends if sends[k] is None}, []

    def link(key):
        return (key[0] ^ key[1], key[2])

    while ready:
        at = min(ready, key=lambda k: (round(max(ready[k], free.get(link(k), 0.0)), 3), -left[k], k))
        since = ready.pop(at)
        begin = max(since, free.get(link(at), 0.0))
        free[link(at)] = begin + PIECE
        order.append((begin, since, at))
        for key, root in sends.items():
            if root == at:
                ready[key] = begin + PIECE + DELAY
    return order


def labels():
    names = {}
    for begin, since, (half, ring, way, s, q) in gather_plan():
        if half == 0:
            names[(ring, way, s + 1, q)] = len(names)
    return names


LABELS = labels()


def route(half, dy, dz):
    off, along = (dz, dy) if half == 0 else (dy, dz)
    if along == 0:
        return None if off == 0 else (0, 1 if off < 0 else -1, abs(off), 0)
    q = OFFS.index(off)
    if along == -4 and UP[q] < 4:
        return (1, -1, 4, q)
    return (1, 1 if along < 0 else -1, abs(along), q)


def gather_steps():
    lands = {(None, 0): 0.0, (None, 1): 0.0}
    for begin, since, (half, ring, way, s, q) in gather_plan():
        lands[((ring, way, s + 1, q), half)] = begin + PIECE + DELAY
    blocks = []
    for dy in OFFS:
        for dz in OFFS:
            blocks.append((max(lands[(route(half, dy, dz), half)] for half in (0, 1)), dy, dz))
    blocks.sort(key=lambda b: (b[0], abs(b[1]) + abs(b[2]), b))
    work, clock = [], READY
    for first in range(0, len(blocks), GROUP):
        group = blocks[first : first + GROUP]
        clock = max(clock, group[-1][0] * 1.15 + 0.5)
        work.append((clock, [b[1:] for b in group]))
        clock = clock + 2 * WORK
    sends = gather_plan()
    merged = []
    marks = [(0.5, "start")] + [(t, "pass") + what for t, what in PASS] + [(t, "work", group) for t, group in work]
    marks.sort(key=lambda m: m[0])
    for mark in marks:
        for entry in [e for e in sends if e[1] * 1.15 + 0.5 <= mark[0] or mark[1] in ('start', 'pass') and e[1] <= mark[0]]:
            merged.append(("send", entry[2]))
            sends.remove(entry)
        merged.append(mark[1:])
    return merged + [("send", entry[2]) for entry in sends]
NLAB = len(LABELS)


def enter(peers, meanwhile=None):
    barrier = pltpu.get_barrier_semaphore()
    for peer in peers:
        pl.semaphore_signal(barrier, inc=1, device_id=peer, device_id_type=MESH)
    if meanwhile is not None:
        meanwhile()
    pl.semaphore_wait(barrier, len(peers))


def ring_peers(y, z, core, x):
    return [neighbour(0, ring, step, y, z, core, x) for ring in (0, 1) for step in (1, -1)]


def group_peers(y, z, core, x):
    me = ctx_of(y, z, core)
    sibling = ctx_of(y, z, 1 - core)
    far = [(me, wrap(x + d, NX)) for d in (1, 2, 3)]
    across = [(sibling, wrap(x + d, NX)) for d in (0, 1, 2, 3)]
    return far, across


def pack_block(block):
    parts = [block[:, 128 * g : 128 * g + 128] for g in range(4)]
    return parts, block[:, VDIM:]


def gather_kernel(
    lat_ref, q_hbm, g_hbm, sel_ref,
    keys_out, q_out, g_out, sel_out, stats_all,
    block, pack, q_ref, g_ref, qrow, grow, stats, unseen,
    load_sem, local_sem, send_sem, recv_sem, gsend, grecv, ssend, srecv,
):
    z, y, core, x = where_am_i()
    chip = y * NZ + z
    load = pltpu.make_async_copy(lat_ref.at[x], block, load_sem)
    load.start()
    load_q = pltpu.make_async_copy(q_hbm, q_ref, local_sem.at[4])
    load_q.start()
    load_g = pltpu.make_async_copy(g_hbm, g_ref, local_sem.at[5])
    load_g.start()
    far, across = group_peers(y, z, core, x)
    def prepare():
        load.wait()
        wide = block[...].astype(F32)
        for g in range(4):
            pack[64 * g : 64 * g + 64, :] = block[:, 128 * g : 128 * g + 128]
        tail = jnp.concatenate([wide[:, VDIM:], jnp.zeros((BLK, 64), F32)], axis=1)
        pack[256:288, :] = (tail[:32] + pltpu.roll(tail[32:], 64, axis=1)).astype(BF16)
        load_q.wait()
        load_g.wait()
        for pair in range(HEADS_HERE // 2):
            both = q_ref[:, 2 * LAT * pair : 2 * LAT * (pair + 1)].astype(F32)
            lane = lax.broadcasted_iota(jnp.int32, (QBLK, WIDE), 1)
            one = jnp.where(lane < LAT, both[:, :WIDE], 0.0)
            two = jnp.where(lane < LAT, pltpu.roll(both[:, VDIM:], WIDE - 64, axis=1), 0.0)
            qrow[16 * pair : 16 * pair + 16, :] = jnp.concatenate([one, two], axis=0).astype(BF16)
            one = g_ref[:, 2 * VDIM * pair : 2 * VDIM * pair + VDIM].astype(F32)
            two = g_ref[:, 2 * VDIM * pair + VDIM : 2 * VDIM * (pair + 1)].astype(F32)
            grow[16 * pair : 16 * pair + 16, :] = jnp.concatenate([one, two], axis=0).astype(BF16)

    enter(ring_peers(y, z, core, x) + far + across, prepare)
    keep = pltpu.make_async_copy(pack, keys_out.at[chip], local_sem.at[0])
    keep.start()

    first = {0: z, 1: y}
    second = {0: y, 1: z}
    sends = []
    arrived = set()

    def part(half):
        return pl.ds(HALF * half, HALF)

    def arrival(half, label):
        if (half, label) in arrived:
            return
        arrived.add((half, label))
        pltpu.make_async_copy(
            keys_out.at[chip, part(half)], keys_out.at[chip, part(half)],
            recv_sem.at[half * NLAB + LABELS[label]],
        ).wait()

    def send(half, ring, way, s, q):
        if ring == 0:
            off, along = -way * s, 0
            if s > 0:
                arrival(half, (0, way, s, 0))
        else:
            off, along = OFFS[q], -way * s
            if s > 0:
                arrival(half, (1, way, s, q))
            elif off != 0:
                arrival(half, (0, 1 if off < 0 else -1, abs(off), 0))
        spot = place(half, wrap(first[half] + off, RING), wrap(second[half] + along, RING))
        own = off == 0 and along == 0
        src = pack.at[part(half)] if own else keys_out.at[spot, part(half)]
        number = half * NLAB + LABELS[(ring, way, s + 1, q)]
        copy = pltpu.make_async_remote_copy(
            src_ref=src,
            dst_ref=keys_out.at[spot, part(half)],
            send_sem=send_sem.at[number],
            recv_sem=recv_sem.at[number],
            device_id=neighbour(half, ring, way, y, z, core, x),
            device_id_type=MESH,
        )
        copy.start()
        sends.append(copy)

    def group_copy(src, out, kind, slot_core, slot_x, peer, number):
        copy = pltpu.make_async_remote_copy(
            src_ref=src,
            dst_ref=out.at[slot_core, slot_x] if kind != 2 else out.at[slot_core],
            send_sem=gsend.at[number],
            recv_sem=grecv.at[number],
            device_id=peer,
            device_id_type=MESH,
        )
        copy.start()
        sends.append(copy)

    group_number = {}

    def number_of(kind, hop):
        return group_number.setdefault((kind, hop), len(group_number))

    def group_arrival(kind, hop):
        ref = (q_out.at[0, 0], g_out.at[0, 0], sel_out.at[0])[kind]
        pltpu.make_async_copy(ref, ref, grecv.at[number_of(kind, hop)]).wait()

    def start_group():
        group_copy(sel_ref, sel_out, 2, core, 0, across[0], number_of(2, 0))
        keep_sel.start()
        group_copy(qrow, q_out, 0, core, x, far[0], number_of(0, 3))
        group_copy(grow, g_out, 1, core, x, far[2], number_of(1, 1))
        group_copy(qrow, q_out, 0, core, x, across[0], number_of(0, 4))
        group_copy(grow, g_out, 1, core, x, across[0], number_of(1, 4))
        group_copy(grow, g_out, 1, core, x, far[0], number_of(1, 3))
        group_copy(qrow, q_out, 0, core, x, far[2], number_of(0, 1))
        keep_q.start()
        keep_g.start()

    def pass_on(kind, hop):
        src_x = wrap(x + hop, NX)
        group_arrival(kind, hop)
        out = (q_out, g_out)[kind]
        if (kind, hop) == (0, 3):
            group_copy(out.at[core, src_x], out, kind, core, src_x, far[0], number_of(kind, 2))
        if (kind, hop) == (1, 1):
            group_copy(out.at[core, src_x], out, kind, core, src_x, far[2], number_of(kind, 2))
        group_copy(out.at[core, src_x], out, kind, core, src_x, across[0], number_of(kind, 4 + hop))

    keep_sel = pltpu.make_async_copy(sel_ref, sel_out.at[core], local_sem.at[1])
    keep_q = pltpu.make_async_copy(qrow, q_out.at[core, x], local_sem.at[2])
    keep_g = pltpu.make_async_copy(grow, g_out.at[core, x], local_sem.at[3])
    def group_done():
        for kind in (0, 1):
            for hop in (4, 5, 6, 7):
                group_arrival(kind, hop)
        group_arrival(2, 0)
        keep_sel.wait()
        keep_q.wait()
        keep_g.wait()
        ids = lax.broadcasted_iota(jnp.int32, (NY * NZ, SLOTS), 0) * 8 + 4 * core + x
        for qb in range(NK):
            hit = jnp.max(jnp.where(sel_out[qb] == ids, 1.0, 0.0), axis=1, keepdims=True)
            unseen[qb] = jnp.broadcast_to(jnp.where(hit > 0.0, 0.0, NEG), (NY * NZ, 128))
            stats[3 * qb : 3 * qb + 3, :] = jnp.concatenate(
                [jnp.full((1, ALLR), NEG, F32), jnp.zeros((2, ALLR), F32)], axis=0
            )

    lane = lax.broadcasted_iota(jnp.int32, (32, 128), 1)

    def work(group):
        fronts, tails, hides = [], [], [[], []]
        for dy, dz in group:
            for half in (0, 1):
                label = route(half, dy, dz)
                if label is not None:
                    arrival(half, label)
            spot = wrap(y + dy, NY) * NZ + wrap(z + dz, NZ)
            if (dy, dz) == (0, 0):
                keep.wait()
            fronts.append(jnp.concatenate([keys_out[spot, 64 * g : 64 * g + 64, :] for g in range(4)], axis=1))
            tail = keys_out[spot, 256:288, :].astype(F32)
            low = jnp.where(lane < 64, tail, 0.0)
            high = jnp.where(lane < 64, pltpu.roll(tail, 64, axis=1), 0.0)
            tails.append(jnp.concatenate([low, high], axis=0).astype(BF16))
            for qb in range(NK):
                hide = jnp.concatenate([unseen[qb, pl.ds(spot, 1), :]] * 4, axis=1)
                hide = jnp.broadcast_to(hide, (BLK, ALLR))
                if (dy, dz) == (0, 0):
                    row = lax.broadcasted_iota(jnp.int32, (BLK, ALLR), 0)
                    col = lax.broadcasted_iota(jnp.int32, (BLK, ALLR), 1)
                    late = row > BLK - QBLK + lax.rem(col, QBLK)
                    own = (x == NX - 1) & (core == qb)
                    hide = jnp.where(late & own, NEG, hide)
                hides[qb].append(hide)
        front = jnp.concatenate(fronts, axis=0)
        whole = jnp.concatenate([front, jnp.concatenate(tails, axis=0)], axis=1)
        scores = [nt(whole, q_out[qb].reshape(ALLR, WIDE)) for qb in range(NK)]
        dprobs = [nt(front, g_out[qb].reshape(ALLR, VDIM)) for qb in range(NK)]
        for qb in range(NK):
            score = SCALE * scores[qb] + jnp.concatenate(hides[qb], axis=0)
            top = stats[3 * qb : 3 * qb + 1, :]
            new_top = jnp.maximum(top, jnp.max(score, axis=0, keepdims=True))
            weights = jnp.exp(score - new_top)
            shrink = jnp.exp(top - new_top)
            total = stats[3 * qb + 1 : 3 * qb + 2, :] * shrink + jnp.sum(weights, axis=0, keepdims=True)
            delta = stats[3 * qb + 2 : 3 * qb + 3, :] * shrink + jnp.sum(weights * dprobs[qb], axis=0, keepdims=True)
            stats[3 * qb : 3 * qb + 3, :] = jnp.concatenate([new_top, total, delta], axis=0)

    stats[...] = jnp.zeros((8, ALLR), F32)
    begun = False
    for mark in gather_steps():
        if mark[0] == "send":
            send(*mark[1])
        elif mark[0] == "start":
            start_group()
        elif mark[0] == "pass":
            pass_on(*mark[1:])
        else:
            if not begun:
                group_done()
                begun = True
            work(*mark[1:])

    slot = x * NK + core
    for number, peer in enumerate(far + across):
        copy = pltpu.make_async_remote_copy(
            src_ref=stats,
            dst_ref=stats_all.at[slot],
            send_sem=ssend.at[number],
            recv_sem=srecv.at[number],
            device_id=peer,
            device_id_type=MESH,
        )
        copy.start()
        sends.append(copy)
    stats_all[slot] = stats[...]
    for number in range(7):
        pltpu.make_async_copy(stats_all.at[0], stats_all.at[0], srecv.at[number]).wait()
    for copy in sends:
        copy.wait_send()


def gather_all(latent, queries, grad_out, selected):
    hbm = pl.BlockSpec(memory_space=pltpu.HBM)
    vmem = pl.BlockSpec(memory_space=pltpu.VMEM)
    return pl.pallas_call(
        gather_kernel,
        out_shape=(
            jax.ShapeDtypeStruct((NY * NZ, ROWS, 128), BF16),
            jax.ShapeDtypeStruct((NK, NX, QR, WIDE), BF16),
            jax.ShapeDtypeStruct((NK, NX, QR, VDIM), BF16),
            jax.ShapeDtypeStruct((NK, 1, SLOTS), jnp.int32),
            jax.ShapeDtypeStruct((NX * NK, 8, ALLR), F32),
        ),
        in_specs=[hbm] * 4,
        out_specs=(vmem,) * 5,
        scratch_shapes=[
            pltpu.VMEM((BLK, LAT), BF16),
            pltpu.VMEM((ROWS, 128), BF16),
            pltpu.VMEM((QBLK, HEADS_HERE * LAT), BF16),
            pltpu.VMEM((QBLK, HEADS_HERE * VDIM), BF16),
            pltpu.VMEM((QR, WIDE), BF16),
            pltpu.VMEM((QR, VDIM), BF16),
            pltpu.VMEM((8, ALLR), F32),
            pltpu.VMEM((NK, NY * NZ, 128), F32),
            pltpu.SemaphoreType.DMA(()),
            pltpu.SemaphoreType.DMA((6,)),
            pltpu.SemaphoreType.DMA((2 * NLAB,)),
            pltpu.SemaphoreType.DMA((2 * NLAB,)),
            pltpu.SemaphoreType.DMA((15,)),
            pltpu.SemaphoreType.DMA((15,)),
            pltpu.SemaphoreType.DMA((7,)),
            pltpu.SemaphoreType.DMA((7,)),
        ],
        compiler_params=pltpu.CompilerParams(
            collective_id=0, has_side_effects=True, vmem_limit_bytes=VMEM_LIMIT
        ),
        cost_estimate=pl.CostEstimate(flops=0, bytes_accessed=10_000_000, transcendentals=0),
        name="gather_keys",
    )(*[pltpu.with_memory_space_constraint(a, pltpu.HBM) for a in (latent, queries, grad_out, selected)])


def list_slots(sel_ref, spots, owns, query_block, kind, own_id):
    def look(j, n):
        block_id = sel_ref[query_block, 0, j]
        mine = (block_id >= 0) & (lax.rem(block_id, 8) == kind)
        spots[n] = jnp.where(mine, block_id // 8, 0)
        owns[n] = jnp.where(mine & (block_id == own_id), 1, 0)
        return n + mine.astype(jnp.int32)

    count = lax.fori_loop(0, SLOTS, look, jnp.int32(0))
    for extra in range(CHUNK):
        spots[count + extra] = 0
        owns[count + extra] = 0
    return count


def take_chunk(chunk, spots, keys_ref, kbuf):
    lane = lax.broadcasted_iota(jnp.int32, (32, 128), 1)
    for i in range(CHUNK):
        spot = spots[chunk * CHUNK + i]
        for g in range(4):
            kbuf[64 * i : 64 * i + 64, 128 * g : 128 * g + 128] = keys_ref[spot, 64 * g : 64 * g + 64, :]
        tail = keys_ref[spot, 256:288, :].astype(F32)
        kbuf[64 * i : 64 * i + 32, VDIM:] = jnp.where(lane < 64, tail, 0.0).astype(BF16)
        kbuf[64 * i + 32 : 64 * i + 64, VDIM:] = jnp.where(
            lane < 64, pltpu.roll(tail, 64, axis=1), 0.0
        ).astype(BF16)


def seen_of(chunk, owns, count):
    row = lax.broadcasted_iota(jnp.int32, (BLK, ALLR), 0)
    col = lax.broadcasted_iota(jnp.int32, (BLK, ALLR), 1)
    limit = BLK - QBLK + lax.rem(col, QBLK)
    parts = []
    for i in range(CHUNK):
        slot = chunk * CHUNK + i
        top = jnp.where(slot < count, jnp.where(owns[slot] == 1, limit, BLK), -1)
        parts.append(row <= top)
    return jnp.concatenate(parts, axis=0)


def nt(a, b):
    return lax.dot_general(a, b, (((1,), (1,)), ((), ())), preferred_element_type=F32)


def tn(a, b):
    return lax.dot_general(a, b, (((0,), (0,)), ((), ())), preferred_element_type=F32)


def nn(a, b):
    return lax.dot_general(a, b, (((1,), (0,)), ((), ())), preferred_element_type=F32)


def grads_kernel(
    sel_ref, keys_ref, q_ref, g_ref, stats_ref, dkeys_ref, dq_ref, kbuf, dq_acc, spots, owns
):
    z, y, core, x = where_am_i()
    chip = y * NZ + z

    def clear(i, carry):
        dkeys_ref[i] = jnp.zeros((ROWS, 128), BF16)
        return carry

    lax.fori_loop(0, NY * NZ, clear, 0)
    for qb in range(NK):
        count = list_slots(sel_ref, spots, owns, qb, 4 * core + x, (chip * NK + qb) * 4 + 3)
        chunks = (count + CHUNK - 1) // CHUNK

        top = stats_ref[0, 3 * qb : 3 * qb + 1, :]
        for d in range(1, NX * NK):
            top = jnp.maximum(top, stats_ref[d, 3 * qb : 3 * qb + 1, :])
        total = jnp.zeros((1, ALLR), F32)
        delta = jnp.zeros((1, ALLR), F32)
        for d in range(NX * NK):
            shrink = jnp.exp(stats_ref[d, 3 * qb : 3 * qb + 1, :] - top)
            total = total + shrink * stats_ref[d, 3 * qb + 1 : 3 * qb + 2, :]
            delta = delta + shrink * stats_ref[d, 3 * qb + 2 : 3 * qb + 3, :]
        inverse = 1.0 / total
        delta = delta * inverse
        dq_acc[...] = jnp.zeros((ALLR, WIDE), F32)

        def step(chunk, carry):
            take_chunk(chunk, spots, keys_ref, kbuf)
            seen = seen_of(chunk, owns, count)
            scores = SCALE * nt(kbuf[...], q_ref[qb])
            dprobs = nt(kbuf[:, :VDIM], g_ref[qb])
            probs = jnp.exp(jnp.where(seen, scores, NEG) - top) * inverse
            probs16 = probs.astype(BF16)
            dscores16 = (probs * (dprobs - delta)).astype(BF16)
            dq_acc[...] += tn(dscores16, kbuf[...])
            dkeys = SCALE * nn(dscores16, q_ref[qb])
            dvalues = nn(probs16, g_ref[qb])
            front = dkeys[:, :VDIM] + dvalues
            back = dkeys[:, VDIM:]
            for i in range(CHUNK):
                slot_now = chunk * CHUNK + i

                @pl.when(slot_now < count)
                def _():
                    spot = spots[slot_now]
                    for g in range(4):
                        old = dkeys_ref[spot, 64 * g : 64 * g + 64, :].astype(F32)
                        new = front[64 * i : 64 * i + 64, 128 * g : 128 * g + 128]
                        dkeys_ref[spot, 64 * g : 64 * g + 64, :] = (old + new).astype(BF16)
                    old = dkeys_ref[spot, 256:288, :].astype(F32)
                    new = back[64 * i : 64 * i + 32] + pltpu.roll(back[64 * i + 32 : 64 * i + 64], 64, axis=1)
                    dkeys_ref[spot, 256:288, :] = (old + new).astype(BF16)

            return carry

        lax.fori_loop(0, chunks, step, 0)
        for g in range(NX):
            dq_ref[qb, g] = (SCALE * dq_acc[QR * g : QR * g + QR, :]).astype(BF16)


def grads_of(sel, keys, queries, grad_out, stats):
    vmem = pl.BlockSpec(memory_space=pltpu.VMEM)
    return pl.pallas_call(
        grads_kernel,
        out_shape=(
            jax.ShapeDtypeStruct((NY * NZ, ROWS, 128), BF16),
            jax.ShapeDtypeStruct((NK, NX, QR, WIDE), BF16),
        ),
        in_specs=[
            pl.BlockSpec(memory_space=pltpu.SMEM),
            vmem,
            vmem,
            vmem,
            vmem,
        ],
        out_specs=(vmem, vmem),
        scratch_shapes=[
            pltpu.VMEM((CK, WIDE), BF16),
            pltpu.VMEM((ALLR, WIDE), F32),
            pltpu.SMEM((SLOTS + CHUNK,), jnp.int32),
            pltpu.SMEM((SLOTS + CHUNK,), jnp.int32),
        ],
        compiler_params=pltpu.CompilerParams(vmem_limit_bytes=VMEM_LIMIT),
        name="local_grads",
    )(sel, keys, queries, grad_out, stats)


def return_kernel(
    dkeys_ref, dq_ref, dq_out, lat_out,
    got, tsum, total, quarters, dq_got, send_sem, recv_sem, qsend, qrecv, lsend, lrecv,
):
    z, y, core, x = where_am_i()
    far, across = group_peers(y, z, core, x)
    peers = far + across
    enter(ring_peers(y, z, core, x) + peers)
    first = {0: z, 1: y}
    second = {0: y, 1: z}
    sends = []

    def part(half):
        return pl.ds(HALF * half, HALF)

    def number(half, ring, way, left, q):
        return half * NLAB + LABELS[(ring, -way, left + 1, q)]

    def arrival(half, ring, way, left, q):
        at = number(half, ring, way, left, q)
        pltpu.make_async_copy(got.at[at], got.at[at], recv_sem.at[at]).wait()
        return at

    def local(half, off, along):
        spot = place(half, wrap(first[half] + off, RING), wrap(second[half] + along, RING))
        return dkeys_ref.at[spot, part(half)]

    def push(src, half, ring, way, left, q):
        at = number(half, ring, way, left, q)
        copy = pltpu.make_async_remote_copy(
            src_ref=src,
            dst_ref=got.at[at],
            send_sem=send_sem.at[at],
            recv_sem=recv_sem.at[at],
            device_id=neighbour(half, ring, way, y, z, core, x),
            device_id_type=MESH,
        )
        copy.start()
        sends.append(copy)

    def row_total(half, q):
        value = local(half, OFFS[q], 0)[...].astype(F32)
        for way in (1, -1):
            at = arrival(half, 1, way, 0, q)
            value = value + got[at].astype(F32)
        return value

    def send_row(half, q):
        off = OFFS[q]
        way, dist = (1, off) if off > 0 else (-1, -off)
        value = row_total(half, q)
        if (0, -way, dist + 1, 0) in LABELS:
            at = arrival(half, 0, way, dist, 0)
            value = value + got[at].astype(F32)
        tsum[half, q] = value.astype(BF16)
        push(tsum.at[half, q], half, 0, way, dist - 1, 0)

    def send_big(half, way, left, q):
        reach = UP[q] if way == -1 else DOWN[q]
        if left == reach - 1:
            push(local(half, OFFS[q], way * (left + 1)), half, 1, way, left, q)
        else:
            at = arrival(half, 1, way, left + 1, q)
            got[at] = (got[at].astype(F32) + local(half, OFFS[q], way * (left + 1))[...].astype(F32)).astype(BF16)
            push(got.at[at], half, 1, way, left, q)

    for turn, (begin, since, (half, ring, way, s, q)) in enumerate(reversed(gather_plan())):
        if ring == 0:
            send_row(half, OFFS.index(-way * (s + 1)))
        else:
            send_big(half, -way, s, q)
        if turn == 24:
            for number_here, (ctx, head) in enumerate(peers):
                to_core = core if number_here < 3 else 1 - core
                copy = pltpu.make_async_remote_copy(
                    src_ref=dq_ref.at[to_core, head],
                    dst_ref=dq_got.at[number_here],
                    send_sem=qsend.at[number_here],
                    recv_sem=qrecv.at[number_here],
                    device_id=(ctx, head),
                    device_id_type=MESH,
                )
                copy.start()
                sends.append(copy)

    for half in (0, 1):
        value = row_total(half, 0)
        for way in (1, -1):
            at = arrival(half, 0, way, 0, 0)
            value = value + got[at].astype(F32)
        total[HALF * half : HALF * half + HALF, :] = value

    lane = lax.broadcasted_iota(jnp.int32, (32, 128), 1)
    tail = total[256:288, :]
    low = jnp.where(lane < 64, tail, 0.0)
    high = jnp.where(lane < 64, pltpu.roll(tail, 64, axis=1), 0.0)
    whole = jnp.concatenate(
        [total[64 * g : 64 * g + 64, :] for g in range(4)] + [jnp.concatenate([low, high], axis=0)], axis=1
    )
    for g in range(NX):
        share = LAT // NX
        turned = whole if g == 0 else pltpu.roll(whole, WIDE - share * g, axis=1)
        quarters[g] = turned[:, :share].astype(BF16)
    for d, peer in enumerate(far):
        copy = pltpu.make_async_remote_copy(
            src_ref=quarters.at[peer[1]],
            dst_ref=lat_out.at[x],
            send_sem=lsend.at[d],
            recv_sem=lrecv.at[d],
            device_id=peer,
            device_id_type=MESH,
        )
        copy.start()
        sends.append(copy)
    lat_out[x] = quarters[x]

    for number_here in range(7):
        pltpu.make_async_copy(
            dq_got.at[number_here], dq_got.at[number_here], qrecv.at[number_here]
        ).wait()
    for pair in range(HEADS_HERE // 2):
        rows = pl.ds(16 * pair, 16)
        value = dq_ref[core, x, rows, :].astype(F32)
        for number_here in range(7):
            value = value + dq_got[number_here, rows, :].astype(F32)
        one, two = value[:QBLK], pltpu.roll(value[QBLK:], 64, axis=1)
        dq_out[:, 2 * LAT * pair : 2 * LAT * (pair + 1)] = jnp.concatenate(
            [one[:, :VDIM], one[:, VDIM:] + two[:, :128], two[:, 128:]], axis=1
        ).astype(BF16)
    for d in range(3):
        pltpu.make_async_copy(lat_out.at[0], lat_out.at[0], lrecv.at[d]).wait()
    for copy in sends:
        copy.wait_send()


def return_all(dkeys, dq):
    vmem = pl.BlockSpec(memory_space=pltpu.VMEM)
    return pl.pallas_call(
        return_kernel,
        out_shape=(
            jax.ShapeDtypeStruct((QBLK, HEADS_HERE * LAT), BF16),
            jax.ShapeDtypeStruct((4, BLK, LAT // NX), BF16),
        ),
        in_specs=[vmem, vmem],
        out_specs=(vmem, vmem),
        scratch_shapes=[
            pltpu.VMEM((2 * NLAB, HALF, 128), BF16),
            pltpu.VMEM((2, len(OFFS), HALF, 128), BF16),
            pltpu.VMEM((ROWS, 128), F32),
            pltpu.VMEM((NX, BLK, LAT // NX), BF16),
            pltpu.VMEM((7, QR, WIDE), BF16),
            pltpu.SemaphoreType.DMA((2 * NLAB,)),
            pltpu.SemaphoreType.DMA((2 * NLAB,)),
            pltpu.SemaphoreType.DMA((7,)),
            pltpu.SemaphoreType.DMA((7,)),
            pltpu.SemaphoreType.DMA((3,)),
            pltpu.SemaphoreType.DMA((3,)),
        ],
        compiler_params=pltpu.CompilerParams(
            collective_id=2, has_side_effects=True, vmem_limit_bytes=VMEM_LIMIT
        ),
        cost_estimate=pl.CostEstimate(flops=0, bytes_accessed=10_000_000, transcendentals=0),
        name="return_grads",
    )(dkeys, dq)


def local(queries, grad_out, latent, selected):
    keys, all_q, all_g, sel, stats = gather_all(latent, queries, grad_out, selected)
    all_q = all_q.reshape(NK, ALLR, WIDE)
    all_g = all_g.reshape(NK, ALLR, VDIM)
    dkeys, dq = grads_of(sel, keys, all_q, all_g, stats)
    return return_all(dkeys, dq)


def solution(mesh):
    placed = (P("ctx", "head"), P("ctx", "head"), P("ctx", None, None), P("ctx", None))
    return jax.shard_map(
        local,
        mesh=mesh,
        in_specs=placed,
        out_specs=(P("ctx", "head"), P("ctx", None, "head")),
        check_vma=False,
    )
```
